32 devices in a mesh: group: 2 (over x), seq: 16 (over z, y, core).
Axes of the slice: x: 2, y: 2, z: 4, core: 2. Of those that a mesh axis runs over, the one named last changes fastest.
Arguments:
- query: bfloat16 [8192, 2048], P(('group', 'seq')), parts along dimension 0, may hold values from -6 to 6
- key_in: bfloat16 [8192, 2048], P(('group', 'seq')), parts along dimension 0, may hold values from -6 to 6
- value: bfloat16 [8192, 2048], P(('group', 'seq')), parts along dimension 0, may hold values from -6 to 6
- d_out: bfloat16 [8192, 2048], P(('group', 'seq')), parts along dimension 0, may hold values from -6 to 6
Outputs:
- output: bfloat16 [8192, 2048], P(('group', 'seq')), parts along dimension 0
- d_query: bfloat16 [8192, 2048], P(('group', 'seq')), parts along dimension 0
- d_key: bfloat16 [8192, 2048], P(('group', 'seq')), parts along dimension 0
- d_value: bfloat16 [8192, 2048], P(('group', 'seq')), parts along dimension 0
The draws below stay inside these ranges and needn't reach their ends.
There are 2 independent parts, one for each index of `group`. The reference program is written for one: setup_inputs(seed, part) draws one part's arguments, and reference() takes and returns one part's arrays. A program takes and returns all parts, laid end to end along the dimension named above; each array names one. Nothing has to cross between parts.
All inputs are finite; a program needn't handle non-finite values.
Results may differ from the reference program's by a relative error of at most 0.0059.
Values sent between devices are 32-bit elements; how exact they have to be, the bound alone decides.
No kernel may reach another device: no remote copies, remote signals or barrier semaphores. Data moves between devices by JAX's collectives and lax.ppermute only.
A program may use at most 320 MiB of HBM per device.

```python
import jax
import jax.numpy as jnp
from jax import lax

H = 16
DH = 128
TOK_DEV = 256
TOKENS = 4096


def block_scale(own_key, dims, pieces, smallest, high):
    def one(dim, parts):
        draws = jax.random.uniform(jax.random.fold_in(jax.random.fold_in(own_key, 6), dim), (parts,), jnp.float32, smallest / len(pieces), high / len(pieces))
        return jnp.repeat(jnp.exp(draws), dims[dim] // parts).reshape((-1,) + (1,) * (len(dims) - dim - 1))

    gain = one(*pieces[0])
    for cut in pieces[1:]:
        gain = gain * one(*cut)
    return gain


def normal_values(stream_key, shape, scale, most, pieces=(), kind=jnp.bfloat16):
    loudness = block_scale(stream_key, shape, pieces, -0.22, 0.18) if pieces else 1.0
    result = jax.random.normal(stream_key, shape, jnp.float32) * scale * loudness
    return jnp.minimum(jnp.maximum(result, -most), most).astype(kind)


def setup_inputs(seed: int = 0, part: int = 0) -> dict:
    key_of = jax.random.split(jax.random.key(seed), 5)
    part_keys = jax.random.split(jax.random.fold_in(key_of[4], part), 5)
    query = normal_values(part_keys[0], (TOKENS, H * DH), 1.0, 6.0, ((0, 16),))
    key_in = normal_values(part_keys[1], (TOKENS, H * DH), 1.0, 6.0, ((0, 16),))
    value = normal_values(part_keys[2], (TOKENS, H * DH), 1.0, 6.0, ((0, 16),))
    d_out = normal_values(part_keys[3], (TOKENS, H * DH), 1.0, 6.0, ((0, 16),))
    return {"query": query, "key_in": key_in, "value": value, "d_out": d_out}


def block_work(items):
    qblk, kblk, vblk, pblk, sblk, gblk, rblk = items
    qf = qblk.astype(jnp.float32)
    kf = kblk.astype(jnp.float32)
    vf = vblk.astype(jnp.float32)
    pf = pblk.astype(jnp.float32)
    sf = sblk.astype(jnp.float32)
    gf = gblk.astype(jnp.float32)
    count = qblk.shape[0]
    lower = jnp.tril(jnp.ones((count, count), jnp.float32))
    scores = (jnp.einsum('thd,shd->hts', qf, kf) * lower).astype(jnp.bfloat16).astype(jnp.float32)
    mixed = jnp.einsum('hts,shd->thd', scores, vf) + jnp.einsum('thd,hde->the', qf, sf)
    output = (mixed * rblk[:, None, None]).astype(jnp.bfloat16)
    back = (jnp.einsum('the,she->hts', pf, vf) * lower).astype(jnp.bfloat16).astype(jnp.float32)
    d_query = (jnp.einsum('hts,shd->thd', back, kf) + jnp.einsum('the,hde->thd', pf, sf)).astype(jnp.bfloat16)
    d_key = (jnp.einsum('hts,thd->shd', back, qf) + jnp.einsum('she,hde->shd', vf, gf)).astype(jnp.bfloat16)
    d_value = (jnp.einsum('hts,the->she', scores, pf) + jnp.einsum('shd,hde->she', kf, gf)).astype(jnp.bfloat16)
    return (output, d_query, d_key, d_value)

def reference(query, key_in, value, d_out):
    blocks = TOKENS // TOK_DEV
    shape = (blocks, TOK_DEV, H, DH)
    qall = query.reshape(shape)
    kall = key_in.reshape(shape)
    vall = value.reshape(shape)
    gall = d_out.reshape(shape)
    where = jnp.arange(TOKENS).reshape(blocks, TOK_DEV).astype(jnp.float32)
    rscale = 1.0 / jnp.sqrt(DH * (where + 1.0))
    scaled = (gall.astype(jnp.float32) * rscale[:, :, None, None]).astype(jnp.bfloat16)
    local_kv = jnp.einsum('bthd,bthe->bhde', kall.astype(jnp.float32), vall.astype(jnp.float32))
    local_qg = jnp.einsum('bthd,bthe->bhde', qall.astype(jnp.float32), scaled.astype(jnp.float32))
    zero_row = jnp.zeros((1, H, DH, DH), jnp.float32)
    kv_state = jnp.concatenate([zero_row, jnp.cumsum(local_kv, axis=0)[:-1]], axis=0).astype(jnp.bfloat16)
    later = jnp.cumsum(local_qg[::-1], axis=0)[::-1]
    grad_state = jnp.concatenate([later[1:], zero_row], axis=0).astype(jnp.bfloat16)
    results = lax.map(block_work, (qall, kall, vall, scaled, kv_state, grad_state, rscale))
    flat = (TOKENS, H * DH)
    return (results[0].reshape(flat), results[1].reshape(flat), results[2].reshape(flat), results[3].reshape(flat))
```

```python
import functools

import jax
import jax.numpy as jnp
from jax import lax
from jax.experimental import pallas as pl
from jax.experimental.pallas import tpu as pltpu
from jax.sharding import PartitionSpec as P

DH = 128
F32 = jnp.float32
BF16 = jnp.bfloat16

CORE, ROW, EVEN, EARLY_KV, START = range(5)


def rows_scale(start, count):
    where = start + lax.broadcasted_iota(jnp.int32, (count, DH), 0)
    return 1.0 / jnp.sqrt(DH * (where.astype(F32) + 1.0))


def dot(a, b, ca, cb):
    return lax.dot_general(a, b, (((ca,), (cb,)), ((), ())), preferred_element_type=F32)


def states_kernel(info, *refs):
    ins, outs = refs[:8], refs[8:12]
    count = ins[0].shape[0]
    scale = rows_scale(info[START], count)
    even = info[EVEN] == 1
    for side in range(2):
        q, k, v, d = ins[4 * side : 4 * side + 4]
        first, second = outs[2 * side : 2 * side + 2]
        for i in range(first.shape[0]):
            cols = slice(i * DH, (i + 1) * DH)
            scaled = (d[:, cols].astype(F32) * scale).astype(BF16)
            kv = dot(k[:, cols], v[:, cols], 0, 0)
            qg = dot(q[:, cols], scaled, 0, 0)
            first[i] = jnp.where(even, kv, qg)
            second[i] = jnp.where(even, qg, kv)


def local_states(info, query, key_in, value, d_out):
    count, width = query.shape
    heads = width // DH
    half, two = heads // 2, 2
    steps = half // two

    def at(side):
        def index(g, info):
            core = info[CORE] if side == 0 else 1 - info[CORE]
            part = g // (steps // 2)
            row = jnp.where(part == 0, info[ROW], 1 - info[ROW])
            return 0, core * steps + row * (steps // 2) + g % (steps // 2)

        return pl.BlockSpec((count, two * DH), index)

    out = pl.BlockSpec((two, DH, DH), lambda g, info: (g, 0, 0))
    args = (query, key_in, value, d_out)
    return pl.pallas_call(
        states_kernel,
        out_shape=[jax.ShapeDtypeStruct((half, DH, DH), F32)] * 4,
        grid_spec=pltpu.PrefetchScalarGridSpec(
            num_scalar_prefetch=1,
            grid=(steps,),
            in_specs=[at(0)] * 4 + [at(1)] * 4,
            out_specs=[out] * 4,
        ),
        compiler_params=pltpu.CompilerParams(vmem_limit_bytes=16 * 2**20),
        name="states",
    )(info, *args, *args)


def final_kernel(info, q, k, v, d, *refs):
    early, late = refs[0:4], refs[4:8]
    o_ref, dq_ref, dk_ref, dv_ref = refs[8:12]
    kv_state, grad_state = refs[12:14]
    g = pl.program_id(0)
    count = q.shape[0]
    steps = pl.num_programs(0)
    early_kv = info[EARLY_KV] == 1
    for kind in range(4):

        @pl.when(g // (steps // 4) == kind)
        def _():
            t, u = early[kind][...], late[kind][...]
            kv_state[...] = jnp.where(early_kv, t, u).astype(BF16)
            grad_state[...] = jnp.where(early_kv, u, t).astype(BF16)

    scale = rows_scale(info[START], count)
    lower = lax.broadcasted_iota(jnp.int32, (count, count), 1) <= lax.broadcasted_iota(
        jnp.int32, (count, count), 0
    )
    for i in range(kv_state.shape[0]):
        cols = slice(i * DH, (i + 1) * DH)
        qh, kh, vh = q[:, cols], k[:, cols], v[:, cols]
        ph = (d[:, cols].astype(F32) * scale).astype(BF16)
        kv, gr = kv_state[i], grad_state[i]
        scores = jnp.where(lower, dot(qh, kh, 1, 1), 0.0).astype(BF16)
        back = jnp.where(lower, dot(ph, vh, 1, 1), 0.0).astype(BF16)
        o_ref[:, cols] = ((dot(scores, vh, 1, 0) + dot(qh, kv, 1, 0)) * scale).astype(BF16)
        dq_ref[:, cols] = (dot(back, kh, 1, 0) + dot(ph, kv, 1, 1)).astype(BF16)
        dk_ref[:, cols] = (dot(back, qh, 0, 0) + dot(vh, gr, 1, 1)).astype(BF16)
        dv_ref[:, cols] = (dot(scores, ph, 0, 0) + dot(kh, gr, 1, 0)).astype(BF16)


def finish(info, query, key_in, value, d_out, early, late):
    count, width = query.shape
    heads = width // DH
    two = 2
    steps = heads // two
    quarter = steps // 4

    def cols(g, info):
        kind = g // quarter
        core = jnp.where(kind < 2, info[CORE], 1 - info[CORE])
        row = jnp.where(kind % 2 == 0, info[ROW], 1 - info[ROW])
        return 0, (core * 2 + row) * quarter + g % quarter

    def state(kind):
        def index(g, info):
            return jnp.clip(g - kind * quarter, 0, quarter - 1), 0, 0

        return pl.BlockSpec((two, DH, DH), index)

    block = pl.BlockSpec((count, two * DH), cols)
    return pl.pallas_call(
        final_kernel,
        out_shape=[jax.ShapeDtypeStruct((count, width), BF16)] * 4,
        grid_spec=pltpu.PrefetchScalarGridSpec(
            num_scalar_prefetch=1,
            grid=(steps,),
            in_specs=[block] * 4 + [state(n) for n in range(4)] * 2,
            out_specs=[block] * 4,
            scratch_shapes=[pltpu.VMEM((two, DH, DH), BF16)] * 2,
        ),
        compiler_params=pltpu.CompilerParams(vmem_limit_bytes=24 * 2**20),
        name="finish",
    )(info, query, key_in, value, d_out, *early, *late)


def send(array, pairs):
    return lax.ppermute(array, "seq", pairs)


def plane_scan(planes, plane, first, second_of):
    def spread(pairs):
        return [(4 * a + i, 4 * b + i) for a, b in pairs for i in range(4)]

    if planes == 4:
        near = send(first, spread([(0, 1), (1, 0), (2, 3), (3, 2)]))
        inner = (plane == 1) | (plane == 2)
        early = jnp.where(inner, near, 0.0)
        middle = send(second_of() + near, spread([(1, 2), (2, 1)]))
        outer = send(middle, spread([(1, 0), (2, 3)]))
        late = middle + outer + jnp.where(inner, 0.0, near)
        return early, late
    even = plane % 2 == 0
    second = second_of()
    kv = jnp.where(even, first, second)
    qg = jnp.where(even, second, first)

    def scan(x, sign):
        def shift(x, by):
            return send(
                x, spread([(a, a + sign * by) for a in range(planes) if 0 <= a + sign * by < planes])
            )

        x, by = shift(x, 1), 1
        while by < planes:
            x, by = x + shift(x, by), 2 * by
        return x

    before, after = scan(kv, 1), scan(qg, -1)
    lower = plane < planes // 2
    return jnp.where(lower, before, after), jnp.where(lower, after, before)


def body(query, key_in, value, d_out):
    count, width = query.shape
    quarter = width // DH // 4
    size, place = lax.axis_size("seq"), lax.axis_index("seq")
    planes = size // 4
    core, row, plane = place % 2, (place // 2) % 2, place // 4
    even = plane % 2 == 0
    early_kv = plane < planes // 2
    info = jnp.stack(
        [core, row, even.astype(jnp.int32), early_kv.astype(jnp.int32), place * count]
    ).astype(jnp.int32)
    core_swap = [(i, i ^ 1) for i in range(size)]
    row_swap = [(i, i ^ 2) for i in range(size)]

    f_own, s_own, f_sib, s_sib = local_states(info, query, key_in, value, d_out)

    def chip_and_plane(own, sib):
        got = send(sib, core_swap)
        keep = own[:quarter] + got[:quarter]
        other = send(own[quarter:] + got[quarter:], row_swap)
        return got, keep, other

    f = chip_and_plane(f_own, f_sib)
    s = chip_and_plane(s_own, s_sib)
    t_val, u_val = plane_scan(planes, plane, f[1] + f[2], lambda: s[1] + s[2])

    first_is_early = even == early_kv

    def spread_out(val, is_first, is_kv):
        own = jnp.where(is_first, f_own, s_own)
        got, keep, other = (jnp.where(is_first, a, b) for a, b in zip(f, s))
        after_row = is_kv == (row == 1)
        d_keep = val + jnp.where(after_row, other, 0.0)
        d_other = send(val + jnp.where(after_row, 0.0, keep), row_swap)
        after_core = is_kv == (core == 1)
        own_states, sib_states = [], []
        for n, d in enumerate((d_keep, d_other)):
            part = slice(n * quarter, (n + 1) * quarter)
            own_states.append(d + jnp.where(after_core, got[part], 0.0))
            sib_states.append(send(d + jnp.where(after_core, 0.0, own[part]), core_swap))
        return own_states + sib_states

    early = spread_out(t_val, first_is_early, early_kv)
    late = spread_out(u_val, ~first_is_early, ~early_kv)
    return tuple(finish(info, query, key_in, value, d_out, early, late))


def solution(mesh):
    spec = P(("group", "seq"), None)
    return jax.shard_map(
        body, mesh=mesh, in_specs=(spec,) * 4, out_specs=(spec,) * 4, check_vma=False
    )
```

```python
import functools

import jax
import jax.numpy as jnp
from jax import lax
from jax.experimental import pallas as pl
from jax.experimental.pallas import tpu as pltpu
from jax.sharding import PartitionSpec as P

DH = 128
F32 = jnp.float32
BF16 = jnp.bfloat16
MIB = 2**20
SMALL = pl.CostEstimate(flops=1, bytes_accessed=1, transcendentals=0)

CORE, ROW, EVEN, EARLY_KV, START, INNER = range(6)

IN_SMEM = pl.BlockSpec(memory_space=pltpu.SMEM)
IN_VMEM = pl.BlockSpec(memory_space=pltpu.VMEM)
IN_HBM = pl.BlockSpec(memory_space=pltpu.HBM)


def rows_scale(start, count):
    where = start + lax.broadcasted_iota(jnp.int32, (count, DH), 0)
    return 1.0 / jnp.sqrt(DH * (where.astype(F32) + 1.0))


def dot(a, b, ca, cb):
    return lax.dot_general(a, b, (((ca,), (cb,)), ((), ())), preferred_element_type=F32)


def first_head(info, side, part, quarter):
    core = info[CORE] if side == 0 else 1 - info[CORE]
    row = info[ROW] if part == 0 else 1 - info[ROW]
    return (core * 2 + row) * quarter


def half_cols(info, side, width):
    core = info[CORE] if side == 0 else 1 - info[CORE]
    half = width // 2
    return pl.multiple_of(core * half, half)


def state_products(is_kv, side, quarter, info, q, k, v, d, out):
    count = q.shape[0]

    @pl.when(is_kv)
    def _():
        for part in range(2):
            head = first_head(info, side, part, quarter)
            for i in range(quarter):
                cols = pl.ds(pl.multiple_of((head + i) * DH, DH), DH)
                out[part * quarter + i] = dot(k[:, cols], v[:, cols], 0, 0)

    @pl.when(jnp.logical_not(is_kv))
    def _():
        scale = rows_scale(info[START], count)
        for part in range(2):
            head = first_head(info, side, part, quarter)
            for i in range(quarter):
                cols = pl.ds(pl.multiple_of((head + i) * DH, DH), DH)
                scaled = (d[:, cols].astype(F32) * scale).astype(BF16)
                out[part * quarter + i] = dot(q[:, cols], scaled, 0, 0)


def pair_copies(info, side, width, rows, sems, *pair):
    half = width // 2
    for n, (there, here) in enumerate(pair):
        for step in range(there.shape[0] // rows):
            at = pl.ds(step * rows, rows), pl.ds(half_cols(info, side, width), half)
            yield pltpu.make_async_copy(there.at[at], here.at[at], sems.at[n, step])


def first_kernel(quarter, rows, info, q, k, v, d, out, left, right, sems):
    width = q.shape[1]
    is_kv = info[EVEN] == 1

    def copies(side, a, b):
        return pair_copies(info, side, width, rows, sems.at[side], (a, left), (b, right))

    @pl.when(is_kv)
    def _():
        for side in (1, 0):
            for copy in copies(side, k, v):
                copy.start()

    @pl.when(jnp.logical_not(is_kv))
    def _():
        for side in (1, 0):
            for copy in copies(side, q, d):
                copy.start()

    for copy in copies(1, k, v):
        copy.wait()
    state_products(is_kv, 1, quarter, info, left, left, right, right, out)
    for copy in copies(0, k, v):
        copy.wait()


def first_state(info, args):
    count, width = args[0].shape
    heads = width // DH
    rows = count // 4
    return pl.pallas_call(
        functools.partial(first_kernel, heads // 4, rows),
        out_shape=[jax.ShapeDtypeStruct((heads // 2, DH, DH), F32)]
        + [jax.ShapeDtypeStruct((count, width), BF16)] * 2,
        in_specs=[IN_SMEM] + [IN_HBM] * 4,
        out_specs=[IN_VMEM] * 3,
        scratch_shapes=[pltpu.SemaphoreType.DMA((2, 2, count // rows))],
        compiler_params=pltpu.CompilerParams(vmem_limit_bytes=4 * MIB),
        cost_estimate=SMALL,
        name="first",
    )(info, *args)


def own_kernel(quarter, info, left, right, out):
    state_products(info[EVEN] == 1, 0, quarter, info, left, left, right, right, out)


def own_state(info, left, right):
    width = left.shape[1]
    heads = width // DH
    return pl.pallas_call(
        functools.partial(own_kernel, heads // 4),
        out_shape=jax.ShapeDtypeStruct((heads // 2, DH, DH), F32),
        in_specs=[IN_SMEM] + [IN_VMEM] * 2,
        out_specs=IN_VMEM,
        compiler_params=pltpu.CompilerParams(vmem_limit_bytes=4 * MIB),
        cost_estimate=SMALL,
        name="own",
    )(info, left, right)


def second_kernel(quarter, rows, n_after, info, q, k, v, d, *refs):
    sib, own, qv, kv, vv, dv, sems = refs[n_after:]
    width = q.shape[1]
    is_kv = info[EVEN] != 1

    def copies(n, side, *pair):
        return pair_copies(info, side, width, rows, sems.at[n], *pair)

    keys, queries = ((k, kv), (v, vv)), ((q, qv), (d, dv))

    def start(*pairs):
        for n, pair in enumerate(pairs):
            for copy in copies(n, 1 - n % 2, *pair):
                copy.start()

    @pl.when(is_kv)
    def _():
        start(keys, keys, queries, queries)

    @pl.when(jnp.logical_not(is_kv))
    def _():
        start(queries, queries, keys, keys)

    for n, out in ((0, sib), (1, own)):
        for copy in copies(n, 1 - n, *keys):
            copy.wait()
        state_products(is_kv, 1 - n, quarter, info, qv, kv, vv, dv, out)
    for n in (2, 3):
        for copy in copies(n, 1 - n % 2, *keys):
            copy.wait()


def second_states(info, args, after):
    count, width = args[0].shape
    heads = width // DH
    rows = count // 4
    return pl.pallas_call(
        functools.partial(second_kernel, heads // 4, rows, len(after)),
        out_shape=[jax.ShapeDtypeStruct((heads // 2, DH, DH), F32)] * 2
        + [jax.ShapeDtypeStruct((count, width), BF16)] * 4,
        in_specs=[IN_SMEM] + [IN_HBM] * 4 + [IN_VMEM] * len(after),
        out_specs=[IN_VMEM] * 6,
        scratch_shapes=[pltpu.SemaphoreType.DMA((4, 2, count // rows))],
        compiler_params=pltpu.CompilerParams(vmem_limit_bytes=4 * MIB),
        cost_estimate=SMALL,
        name="second",
    )(info, *args, *after)


def local_kernel(side, quarter, n_after, info, q, k, v, d, *refs):
    o_ref, dq_ref, dk_ref, dv_ref, zero = refs[n_after:]
    zero[...] = jnp.zeros_like(zero)
    count = q.shape[0]
    two = 2
    scale = rows_scale(info[START], count)
    lower = lax.broadcasted_iota(jnp.int32, (count, count), 1) <= lax.broadcasted_iota(
        jnp.int32, (count, count), 0
    )

    for part in range(2):
        first = first_head(info, side, part, quarter)

        def step(g, carry):
            for i in range(two):
                to = pl.ds(pl.multiple_of((part * quarter + g * two + i) * DH, DH), DH)
                cols = pl.ds(pl.multiple_of((first + g * two + i) * DH, DH), DH)
                qh, kh, vh = q[:, cols], k[:, cols], v[:, cols]
                ph = (d[:, cols].astype(F32) * scale).astype(BF16)
                scores = jnp.where(lower, dot(qh, kh, 1, 1), 0.0).astype(BF16)
                back = jnp.where(lower, dot(ph, vh, 1, 1), 0.0).astype(BF16)
                o_ref[:, to] = dot(scores, vh, 1, 0)
                dq_ref[:, to] = dot(back, kh, 1, 0)
                dk_ref[:, to] = dot(back, qh, 0, 0)
                dv_ref[:, to] = dot(scores, ph, 0, 0)
            return carry

        lax.fori_loop(0, quarter // two, step, 0)


def local_part(info, args, side, after=()):
    count, width = args[0].shape
    quarter = width // DH // 4
    *partials, zero = pl.pallas_call(
        functools.partial(local_kernel, side, quarter, len(after)),
        out_shape=[jax.ShapeDtypeStruct((count, width // 2), F32)] * 4
        + [jax.ShapeDtypeStruct((quarter, DH, DH), F32)],
        in_specs=[IN_SMEM] + [IN_VMEM] * (4 + len(after)),
        out_specs=[IN_VMEM] * 5,
        compiler_params=pltpu.CompilerParams(vmem_limit_bytes=8 * MIB),
        cost_estimate=SMALL,
        name="local",
    )(info, *args, *after)
    return partials, zero


def apply_kernel(early, kinds, sides, quarter, n_filled, n_after, info, *refs):
    q, k, v, d = refs[:4]
    refs = refs[4:]
    partials = {side: refs[4 * n : 4 * n + 4] for n, side in enumerate(sides)}
    refs = refs[4 * len(sides) :]
    state_refs, refs = refs[: len(kinds)], refs[len(kinds) + n_filled + n_after :]
    o_hbm, dq_hbm, dk_hbm, dv_hbm, zero, one, other, sems = refs
    zero[...] = jnp.zeros_like(zero)
    count = q.shape[0]
    two = 2
    is_kv = (info[EARLY_KV] == 1) if early else (info[EARLY_KV] != 1)
    steps = [(n, j) for n in range(len(kinds)) for j in range(quarter // two)]
    starts = [first_head(info, side, part, quarter) * DH for side, part in kinds]

    def columns(n, head):
        return pl.multiple_of(starts[n] + head * DH, DH)

    def copies(step, a, b):
        n, j = steps[step]
        here = pl.ds(step * two * DH, two * DH)
        there = pl.ds(pl.multiple_of(starts[n] + j * two * DH, two * DH), two * DH)
        return (
            pltpu.make_async_copy(one.at[:, here], a.at[:, there], sems.at[step, 0]),
            pltpu.make_async_copy(other.at[:, here], b.at[:, there], sems.at[step, 1]),
        )

    def each_head(products, a, b):
        for step, (n, j) in enumerate(steps):
            side, part = kinds[n]
            for i in range(two):
                head = j * two + i
                cols = pl.ds(columns(n, head), DH)
                at = (part * quarter + head) * DH
                here = slice((step * two + i) * DH, (step * two + i + 1) * DH)
                one[:, here], other[:, here] = products(
                    cols, partials[side], slice(at, at + DH), state_refs[n][head].astype(BF16)
                )
            for copy in copies(step, a, b):
                copy.start()

    @pl.when(is_kv)
    def _():
        scale = rows_scale(info[START], count)

        def products(cols, partial, at, kv):
            o_part, dq_part = partial[0][:, at], partial[1][:, at]
            ph = (d[:, cols].astype(F32) * scale).astype(BF16)
            return (
                ((o_part + dot(q[:, cols], kv, 1, 0)) * scale).astype(BF16),
                (dq_part + dot(ph, kv, 1, 1)).astype(BF16),
            )

        each_head(products, o_hbm, dq_hbm)

    @pl.when(jnp.logical_not(is_kv))
    def _():
        def products(cols, partial, at, gr):
            dk_part, dv_part = partial[2][:, at], partial[3][:, at]
            return (
                (dk_part + dot(v[:, cols], gr, 1, 1)).astype(BF16),
                (dv_part + dot(k[:, cols], gr, 1, 0)).astype(BF16),
            )

        each_head(products, dk_hbm, dv_hbm)

    for step in range(len(steps)):
        for copy in copies(step, o_hbm, dq_hbm):
            copy.wait()


def apply_states(info, args, partials, early, kinds, arrays, outs, after=()):
    count, width = args[0].shape
    quarter = width // DH // 4
    filled = () if outs is None else tuple(outs)
    sides = sorted({side for side, _ in kinds})
    partials = [x for side in sides for x in partials[side]]
    first_out = 5 + len(partials) + len(kinds)
    columns = len(kinds) * quarter * DH
    return pl.pallas_call(
        functools.partial(
            apply_kernel, early, kinds, sides, quarter, len(filled), len(after)
        ),
        out_shape=[jax.ShapeDtypeStruct((count, width), BF16)] * 4
        + [jax.ShapeDtypeStruct((quarter, DH, DH), F32)],
        in_specs=[IN_SMEM]
        + [IN_VMEM] * (4 + len(partials) + len(kinds))
        + [IN_HBM] * len(filled)
        + [IN_VMEM] * len(after),
        out_specs=[IN_HBM] * 4 + [IN_VMEM],
        scratch_shapes=[
            pltpu.VMEM((count, columns), BF16),
            pltpu.VMEM((count, columns), BF16),
            pltpu.SemaphoreType.DMA((columns // (2 * DH), 2)),
        ],
        input_output_aliases={first_out + n: n for n in range(len(filled))},
        compiler_params=pltpu.CompilerParams(vmem_limit_bytes=8 * MIB),
        cost_estimate=SMALL,
        name="apply",
    )(info, *args, *partials, *arrays, *filled, *after)


def prepare_kernel(early, n_after, info, *refs):
    near, f_own, f_got, f_keep, f_other, s_own, s_got, s_keep, s_other = refs[:9]
    across, mine, theirs, rest_mine, rest_theirs = refs[9 + n_after :]
    quarter = near.shape[0]
    is_kv = (info[EARLY_KV] == 1) if early else (info[EARLY_KV] != 1)
    is_first = (info[EVEN] == 1) == is_kv
    takes_near = (info[INNER] == 1) if early else (info[INNER] != 1)
    after_row = is_kv == (info[ROW] == 1)
    after_core = is_kv == (info[CORE] == 1)
    for i in range(quarter):
        val = jnp.where(takes_near, near[i], 0.0)
        keep = jnp.where(is_first, f_keep[i], s_keep[i])
        other = jnp.where(is_first, f_other[i], s_other[i])
        own = jnp.where(is_first, f_own[i], s_own[i])
        got = jnp.where(is_first, f_got[i], s_got[i])
        across[i] = val + jnp.where(after_row, 0.0, keep)
        here = val + jnp.where(after_row, other, 0.0)
        mine[i] = here + jnp.where(after_core, got, 0.0)
        theirs[i] = here + jnp.where(after_core, 0.0, own)
        own = jnp.where(is_first, f_own[quarter + i], s_own[quarter + i])
        got = jnp.where(is_first, f_got[quarter + i], s_got[quarter + i])
        rest_mine[i] = jnp.where(after_core, got, 0.0)
        rest_theirs[i] = jnp.where(after_core, 0.0, own)


def prepare(info, early, near, f, s, after):
    return pl.pallas_call(
        functools.partial(prepare_kernel, early, len(after)),
        out_shape=[jax.ShapeDtypeStruct(near.shape, F32)] * 5,
        in_specs=[IN_SMEM] + [IN_VMEM] * (9 + len(after)),
        out_specs=[IN_VMEM] * 5,
        compiler_params=pltpu.CompilerParams(vmem_limit_bytes=4 * MIB),
        cost_estimate=SMALL,
        name="prepare",
    )(info, near, *f, *s, *after)


def send(array, pairs):
    return lax.ppermute(array, "seq", pairs)


def plane_scan(planes, kv, qg):
    def scan(x, sign):
        def shift(x, by):
            pairs = [(a, a + sign * by) for a in range(planes) if 0 <= a + sign * by < planes]
            return send(x, spread_pairs(pairs))

        x, by = shift(x, 1), 1
        while by < planes:
            x, by = x + shift(x, by), 2 * by
        return x

    return scan(kv, 1), scan(qg, -1)


def spread_pairs(pairs):
    return [(4 * a + i, 4 * b + i) for a, b in pairs for i in range(4)]


def body(query, key_in, value, d_out):
    args = (query, key_in, value, d_out)
    count, width = query.shape
    heads = width // DH
    size, place = lax.axis_size("seq"), lax.axis_index("seq")
    planes = size // 4
    core, row, plane = place % 2, (place // 2) % 2, place // 4
    even = plane % 2 == 0
    early_kv = plane < planes // 2
    inner = (plane == 1) | (plane == 2) | (planes != 4)
    info = jnp.stack([core, row, even, early_kv, place * count, inner]).astype(jnp.int32)
    core_swap = [(i, i ^ 1) for i in range(size)]
    row_swap = [(i, i ^ 2) for i in range(size)]
    far_args = tuple(pltpu.with_memory_space_constraint(x, pltpu.HBM) for x in args)

    quarter = heads // 4

    def halves(own, got):
        return own[:quarter] + got[:quarter], own[quarter:] + got[quarter:]

    f_sib, left, right = first_state(info, far_args)
    f_got = send(f_sib, core_swap)
    f_own = own_state(info, left, right)
    f_keep, f_give = halves(f_own, f_got)
    f_other = send(f_give, row_swap)
    s_sib, s_own, *args = second_states(info, far_args, (f_give,))
    s_sib, f_other = lax.optimization_barrier((s_sib, f_other))
    s_got = send(s_sib, core_swap)
    s_keep, s_give = halves(s_own, s_got)
    s_other = send(s_give, row_swap)
    f_total = f_keep + f_other
    f = f_own, f_got, f_keep, f_other
    s = s_own, s_got, s_keep, s_other
    half_a, zero = local_part(info, args, 0, (s_give,))
    half_b, zero = local_part(info, args, 1, (zero,))
    partials = half_a, half_b
    if planes == 4:
        near = send(f_total, spread_pairs([(0, 1), (1, 0), (2, 3), (3, 2)]))
        pair = s_keep + s_other + near + zero
        far = send(pair, spread_pairs([(1, 3), (2, 0)]))
        middle = send(pair, spread_pairs([(1, 2), (2, 1)]))
        coming = far + middle
    else:
        s_total = s_keep + s_other + zero
        kv, qg = plane_scan(
            planes, jnp.where(even, f_total, s_total), jnp.where(even, s_total, f_total)
        )
        near = pair = jnp.where(early_kv, kv, qg)
        coming = jnp.where(early_kv, qg, kv)
    across, mine, theirs, rest_mine, rest_theirs = prepare(info, True, near, f, s, ())

    finish = functools.partial(apply_states, info, args, partials)
    kept_heads, other_heads = ((0, 0), (1, 0)), ((0, 1), (1, 1))
    t_other = send(across, row_swap)
    t_kept = mine, send(theirs, core_swap)
    late = prepare(info, False, near, f, s, (across,))
    *outs, zero = finish(True, kept_heads, t_kept, None, (across, late[0]))
    t_rest = t_other + rest_mine + zero, send(t_other + rest_theirs, core_swap)

    across, mine, theirs = (coming + x for x in late[:3])
    u_other = send(across, row_swap)
    u_kept = mine, send(theirs, core_swap)
    *outs, _ = finish(True, other_heads, t_rest, outs, (across,))
    *outs, zero = finish(False, kept_heads, u_kept, outs)
    u_rest = u_other + late[3] + zero, send(u_other + late[4], core_swap)
    *outs, _ = finish(False, other_heads, u_rest, outs)
    return tuple(outs)


def solution(mesh):
    spec = P(("group", "seq"), None)
    return jax.shard_map(
        body, mesh=mesh, in_specs=(spec,) * 4, out_specs=(spec,) * 4, check_vma=False
    )
```

```python
import functools

import jax
import jax.numpy as jnp
from jax import lax
from jax.experimental import pallas as pl
from jax.experimental.pallas import tpu as pltpu
from jax.sharding import PartitionSpec as P

DH = 128
F32 = jnp.float32
BF16 = jnp.bfloat16
MIB = 2**20
SMALL = pl.CostEstimate(flops=1, bytes_accessed=1, transcendentals=0)

CORE, ROW, EVEN, EARLY_KV, START, INNER = range(6)

IN_SMEM = pl.BlockSpec(memory_space=pltpu.SMEM)
IN_VMEM = pl.BlockSpec(memory_space=pltpu.VMEM)
IN_HBM = pl.BlockSpec(memory_space=pltpu.HBM)


def rows_scale(start, count):
    where = start + lax.broadcasted_iota(jnp.int32, (count, DH), 0)
    return 1.0 / jnp.sqrt(DH * (where.astype(F32) + 1.0))


def dot(a, b, ca, cb):
    return lax.dot_general(a, b, (((ca,), (cb,)), ((), ())), preferred_element_type=F32)


def first_head(info, side, part, quarter):
    core = info[CORE] if side == 0 else 1 - info[CORE]
    row = info[ROW] if part == 0 else 1 - info[ROW]
    return (core * 2 + row) * quarter


def half_cols(info, side, width):
    core = info[CORE] if side == 0 else 1 - info[CORE]
    half = width // 2
    return pl.multiple_of(core * half, half)


def state_products(is_kv, side, quarter, info, q, k, v, d, out):
    count = q.shape[0]

    @pl.when(is_kv)
    def _():
        for part in range(2):
            head = first_head(info, side, part, quarter)
            for i in range(quarter):
                cols = pl.ds(pl.multiple_of((head + i) * DH, DH), DH)
                out[part * quarter + i] = dot(k[:, cols], v[:, cols], 0, 0)

    @pl.when(jnp.logical_not(is_kv))
    def _():
        scale = rows_scale(info[START], count)
        for part in range(2):
            head = first_head(info, side, part, quarter)
            for i in range(quarter):
                cols = pl.ds(pl.multiple_of((head + i) * DH, DH), DH)
                scaled = (d[:, cols].astype(F32) * scale).astype(BF16)
                out[part * quarter + i] = dot(q[:, cols], scaled, 0, 0)


def pair_copies(info, side, width, rows, sems, *pair):
    half = width // 2
    for n, (there, here) in enumerate(pair):
        for step in range(there.shape[0] // rows):
            at = pl.ds(step * rows, rows), pl.ds(half_cols(info, side, width), half)
            yield pltpu.make_async_copy(there.at[at], here.at[at], sems.at[n, step])


def first_kernel(quarter, rows, info, q, k, v, d, out, left, right, sems):
    width = q.shape[1]
    is_kv = info[EVEN] == 1

    def copies(side, a, b):
        return pair_copies(info, side, width, rows, sems.at[side], (a, left), (b, right))

    @pl.when(is_kv)
    def _():
        for side in (1, 0):
            for copy in copies(side, k, v):
                copy.start()

    @pl.when(jnp.logical_not(is_kv))
    def _():
        for side in (1, 0):
            for copy in copies(side, q, d):
                copy.start()

    for copy in copies(1, k, v):
        copy.wait()
    state_products(is_kv, 1, quarter, info, left, left, right, right, out)
    for copy in copies(0, k, v):
        copy.wait()


def first_state(info, args):
    count, width = args[0].shape
    heads = width // DH
    rows = count // 4
    return pl.pallas_call(
        functools.partial(first_kernel, heads // 4, rows),
        out_shape=[jax.ShapeDtypeStruct((heads // 2, DH, DH), F32)]
        + [jax.ShapeDtypeStruct((count, width), BF16)] * 2,
        in_specs=[IN_SMEM] + [IN_HBM] * 4,
        out_specs=[IN_VMEM] * 3,
        scratch_shapes=[pltpu.SemaphoreType.DMA((2, 2, count // rows))],
        compiler_params=pltpu.CompilerParams(vmem_limit_bytes=4 * MIB),
        cost_estimate=SMALL,
        name="first",
    )(info, *args)


def own_kernel(quarter, info, left, right, out):
    state_products(info[EVEN] == 1, 0, quarter, info, left, left, right, right, out)


def own_state(info, left, right):
    width = left.shape[1]
    heads = width // DH
    return pl.pallas_call(
        functools.partial(own_kernel, heads // 4),
        out_shape=jax.ShapeDtypeStruct((heads // 2, DH, DH), F32),
        in_specs=[IN_SMEM] + [IN_VMEM] * 2,
        out_specs=IN_VMEM,
        compiler_params=pltpu.CompilerParams(vmem_limit_bytes=4 * MIB),
        cost_estimate=SMALL,
        name="own",
    )(info, left, right)


def second_kernel(quarter, rows, n_after, info, q, k, v, d, *refs):
    sib, own, qv, kv, vv, dv, sems = refs[n_after:]
    width = q.shape[1]
    is_kv = info[EVEN] != 1

    def copies(n, side, *pair):
        return pair_copies(info, side, width, rows, sems.at[n], *pair)

    keys, queries = ((k, kv), (v, vv)), ((q, qv), (d, dv))

    def start(*pairs):
        for n, pair in enumerate(pairs):
            for copy in copies(n, 1 - n % 2, *pair):
                copy.start()

    @pl.when(is_kv)
    def _():
        start(keys, keys, queries, queries)

    @pl.when(jnp.logical_not(is_kv))
    def _():
        start(queries, queries, keys, keys)

    for n, out in ((0, sib), (1, own)):
        for copy in copies(n, 1 - n, *keys):
            copy.wait()
        state_products(is_kv, 1 - n, quarter, info, qv, kv, vv, dv, out)
    for n in (2, 3):
        for copy in copies(n, 1 - n % 2, *keys):
            copy.wait()


def second_states(info, args, after):
    count, width = args[0].shape
    heads = width // DH
    rows = count // 4
    return pl.pallas_call(
        functools.partial(second_kernel, heads // 4, rows, len(after)),
        out_shape=[jax.ShapeDtypeStruct((heads // 2, DH, DH), F32)] * 2
        + [jax.ShapeDtypeStruct((count, width), BF16)] * 4,
        in_specs=[IN_SMEM] + [IN_HBM] * 4 + [IN_VMEM] * len(after),
        out_specs=[IN_VMEM] * 6,
        scratch_shapes=[pltpu.SemaphoreType.DMA((4, 2, count // rows))],
        compiler_params=pltpu.CompilerParams(vmem_limit_bytes=4 * MIB),
        cost_estimate=SMALL,
        name="second",
    )(info, *args, *after)


def local_kernel(side, quarter, mark, n_after, info, q, k, v, d, *refs):
    o_ref, dq_ref, dk_ref, dv_ref, zero = refs[n_after:]
    zero[...] = jnp.full(zero.shape, jnp.where(info[INNER] == 1, mark, 0.0), F32)
    count = q.shape[0]
    two = 2
    scale = rows_scale(info[START], count)
    lower = lax.broadcasted_iota(jnp.int32, (count, count), 1) <= lax.broadcasted_iota(
        jnp.int32, (count, count), 0
    )

    for part in range(2):
        first = first_head(info, side, part, quarter)

        def step(g, carry):
            for i in range(two):
                to = pl.ds(pl.multiple_of((part * quarter + g * two + i) * DH, DH), DH)
                cols = pl.ds(pl.multiple_of((first + g * two + i) * DH, DH), DH)
                qh, kh, vh = q[:, cols], k[:, cols], v[:, cols]
                ph = (d[:, cols].astype(F32) * scale).astype(BF16)
                scores = jnp.where(lower, dot(qh, kh, 1, 1), 0.0).astype(BF16)
                back = jnp.where(lower, dot(ph, vh, 1, 1), 0.0).astype(BF16)
                o_ref[:, to] = dot(scores, vh, 1, 0)
                dq_ref[:, to] = dot(back, kh, 1, 0)
                dk_ref[:, to] = dot(back, qh, 0, 0)
                dv_ref[:, to] = dot(scores, ph, 0, 0)
            return carry

        lax.fori_loop(0, quarter // two, step, 0)


def local_part(info, args, side, mark, after=()):
    count, width = args[0].shape
    quarter = width // DH // 4
    *partials, zero = pl.pallas_call(
        functools.partial(local_kernel, side, quarter, mark, len(after)),
        out_shape=[jax.ShapeDtypeStruct((count, width // 2), F32)] * 4
        + [jax.ShapeDtypeStruct((quarter, DH, DH), F32)],
        in_specs=[IN_SMEM] + [IN_VMEM] * (4 + len(after)),
        out_specs=[IN_VMEM] * 5,
        compiler_params=pltpu.CompilerParams(vmem_limit_bytes=8 * MIB),
        cost_estimate=SMALL,
        name="local",
    )(info, *args, *after)
    return partials, zero


def apply_kernel(early, kinds, sides, quarter, n_filled, n_after, info, *refs):
    q, k, v, d = refs[:4]
    refs = refs[4:]
    partials = {side: refs[4 * n : 4 * n + 4] for n, side in enumerate(sides)}
    refs = refs[4 * len(sides) :]
    state_refs, refs = refs[: len(kinds)], refs[len(kinds) + n_filled + n_after :]
    o_hbm, dq_hbm, dk_hbm, dv_hbm, zero, one, other, sems = refs
    zero[...] = jnp.zeros_like(zero)
    count = q.shape[0]
    two = 2
    is_kv = (info[EARLY_KV] == 1) if early else (info[EARLY_KV] != 1)
    steps = [(n, j) for n in range(len(kinds)) for j in range(quarter // two)]
    starts = [first_head(info, side, part, quarter) * DH for side, part in kinds]

    def columns(n, head):
        return pl.multiple_of(starts[n] + head * DH, DH)

    def copies(step, a, b):
        n, j = steps[step]
        here = pl.ds(step * two * DH, two * DH)
        there = pl.ds(pl.multiple_of(starts[n] + j * two * DH, two * DH), two * DH)
        return (
            pltpu.make_async_copy(one.at[:, here], a.at[:, there], sems.at[step, 0]),
            pltpu.make_async_copy(other.at[:, here], b.at[:, there], sems.at[step, 1]),
        )

    def each_head(products, a, b):
        for step, (n, j) in enumerate(steps):
            side, part = kinds[n]
            for i in range(two):
                head = j * two + i
                cols = pl.ds(columns(n, head), DH)
                at = (part * quarter + head) * DH
                here = slice((step * two + i) * DH, (step * two + i + 1) * DH)
                one[:, here], other[:, here] = products(
                    cols, partials[side], slice(at, at + DH), state_refs[n][head].astype(BF16)
                )
            for copy in copies(step, a, b):
                copy.start()

    @pl.when(is_kv)
    def _():
        scale = rows_scale(info[START], count)

        def products(cols, partial, at, kv):
            o_part, dq_part = partial[0][:, at], partial[1][:, at]
            ph = (d[:, cols].astype(F32) * scale).astype(BF16)
            return (
                ((o_part + dot(q[:, cols], kv, 1, 0)) * scale).astype(BF16),
                (dq_part + dot(ph, kv, 1, 1)).astype(BF16),
            )

        each_head(products, o_hbm, dq_hbm)

    @pl.when(jnp.logical_not(is_kv))
    def _():
        def products(cols, partial, at, gr):
            dk_part, dv_part = partial[2][:, at], partial[3][:, at]
            return (
                (dk_part + dot(v[:, cols], gr, 1, 1)).astype(BF16),
                (dv_part + dot(k[:, cols], gr, 1, 0)).astype(BF16),
            )

        each_head(products, dk_hbm, dv_hbm)

    for step in range(len(steps)):
        for copy in copies(step, o_hbm, dq_hbm):
            copy.wait()


def apply_states(info, args, partials, early, kinds, arrays, outs, after=()):
    count, width = args[0].shape
    quarter = width // DH // 4
    filled = () if outs is None else tuple(outs)
    sides = sorted({side for side, _ in kinds})
    partials = [x for side in sides for x in partials[side]]
    first_out = 5 + len(partials) + len(kinds)
    columns = len(kinds) * quarter * DH
    return pl.pallas_call(
        functools.partial(
            apply_kernel, early, kinds, sides, quarter, len(filled), len(after)
        ),
        out_shape=[jax.ShapeDtypeStruct((count, width), BF16)] * 4
        + [jax.ShapeDtypeStruct((quarter, DH, DH), F32)],
        in_specs=[IN_SMEM]
        + [IN_VMEM] * (4 + len(partials) + len(kinds))
        + [IN_HBM] * len(filled)
        + [IN_VMEM] * len(after),
        out_specs=[IN_HBM] * 4 + [IN_VMEM],
        scratch_shapes=[
            pltpu.VMEM((count, columns), BF16),
            pltpu.VMEM((count, columns), BF16),
            pltpu.SemaphoreType.DMA((columns // (2 * DH), 2)),
        ],
        input_output_aliases={first_out + n: n for n in range(len(filled))},
        compiler_params=pltpu.CompilerParams(vmem_limit_bytes=8 * MIB),
        cost_estimate=SMALL,
        name="apply",
    )(info, *args, *partials, *arrays, *filled, *after)


def prepare_kernel(early, n_after, info, *refs):
    near, f_own, f_got, f_keep, f_other, s_own, s_got, s_keep, s_other = refs[:9]
    across, mine, theirs, rest_mine, rest_theirs = refs[9 + n_after :]
    quarter = near.shape[0]
    is_kv = (info[EARLY_KV] == 1) if early else (info[EARLY_KV] != 1)
    is_first = (info[EVEN] == 1) == is_kv
    takes_near = (info[INNER] == 1) if early else (info[INNER] != 1)
    after_row = is_kv == (info[ROW] == 1)
    after_core = is_kv == (info[CORE] == 1)
    for i in range(quarter):
        val = jnp.where(takes_near, near[i], 0.0)
        keep = jnp.where(is_first, f_keep[i], s_keep[i])
        other = jnp.where(is_first, f_other[i], s_other[i])
        own = jnp.where(is_first, f_own[i], s_own[i])
        got = jnp.where(is_first, f_got[i], s_got[i])
        across[i] = val + jnp.where(after_row, 0.0, keep)
        here = val + jnp.where(after_row, other, 0.0)
        mine[i] = here + jnp.where(after_core, got, 0.0)
        theirs[i] = here + jnp.where(after_core, 0.0, own)
        own = jnp.where(is_first, f_own[quarter + i], s_own[quarter + i])
        got = jnp.where(is_first, f_got[quarter + i], s_got[quarter + i])
        rest_mine[i] = jnp.where(after_core, got, 0.0)
        rest_theirs[i] = jnp.where(after_core, 0.0, own)


def prepare(info, early, near, f, s, after):
    return pl.pallas_call(
        functools.partial(prepare_kernel, early, len(after)),
        out_shape=[jax.ShapeDtypeStruct(near.shape, F32)] * 5,
        in_specs=[IN_SMEM] + [IN_VMEM] * (9 + len(after)),
        out_specs=[IN_VMEM] * 5,
        compiler_params=pltpu.CompilerParams(vmem_limit_bytes=4 * MIB),
        cost_estimate=SMALL,
        name="prepare",
    )(info, near, *f, *s, *after)


def send(array, pairs):
    return lax.ppermute(array, "seq", pairs)


def plane_scan(planes, kv, qg):
    def scan(x, sign):
        def shift(x, by):
            pairs = [(a, a + sign * by) for a in range(planes) if 0 <= a + sign * by < planes]
            return send(x, spread_pairs(pairs))

        x, by = shift(x, 1), 1
        while by < planes:
            x, by = x + shift(x, by), 2 * by
        return x

    return scan(kv, 1), scan(qg, -1)


def spread_pairs(pairs):
    return [(4 * a + i, 4 * b + i) for a, b in pairs for i in range(4)]


def body(query, key_in, value, d_out):
    args = (query, key_in, value, d_out)
    count, width = query.shape
    heads = width // DH
    size, place = lax.axis_size("seq"), lax.axis_index("seq")
    planes = size // 4
    core, row, plane = place % 2, (place // 2) % 2, place // 4
    even = plane % 2 == 0
    early_kv = plane < planes // 2
    inner = (plane == 1) | (plane == 2) | (planes != 4)
    info = jnp.stack([core, row, even, early_kv, place * count, inner]).astype(jnp.int32)
    core_swap = [(i, i ^ 1) for i in range(size)]
    row_swap = [(i, i ^ 2) for i in range(size)]
    far_args = tuple(pltpu.with_memory_space_constraint(x, pltpu.HBM) for x in args)

    quarter = heads // 4

    def halves(own, got):
        return own[:quarter] + got[:quarter], own[quarter:] + got[quarter:]

    f_sib, left, right = first_state(info, far_args)
    f_got = send(f_sib, core_swap)
    f_own = own_state(info, left, right)
    f_keep, f_give = halves(f_own, f_got)
    f_other = send(f_give, row_swap)
    s_sib, s_own, *args = second_states(info, far_args, (f_give,))
    half_a, zero = local_part(info, args, 0, 0.0, (s_own,))
    s_sib, f_other, zero = lax.optimization_barrier((s_sib, f_other, zero))
    s_got = send(s_sib, core_swap)
    s_keep, s_give = halves(s_own, s_got)
    s_other = send(s_give, row_swap)
    f_total = f_keep + f_other + zero
    f = f_own, f_got, f_keep, f_other
    s = s_own, s_got, s_keep, s_other
    half_b, inside = local_part(info, args, 1, 1.0, (s_give,))
    partials = half_a, half_b
    if planes == 4:
        near = send(f_total, spread_pairs([(0, 1), (1, 0), (2, 3), (3, 2)]))
        pair = jnp.where(inside > 0.0, s_keep + s_other + near, 0.0)
        middle = send(pair, spread_pairs([(1, 2), (2, 1)]) + core_swap[:4] + core_swap[-4:])
        outer = send(middle, spread_pairs([(0, 1), (1, 0), (2, 3), (3, 2)]))
        coming = middle + outer
    else:
        s_total = s_keep + s_other
        kv, qg = plane_scan(
            planes, jnp.where(even, f_total, s_total), jnp.where(even, s_total, f_total)
        )
        near = pair = jnp.where(early_kv, kv, qg)
        coming = jnp.where(early_kv, qg, kv)
    across, mine, theirs, rest_mine, rest_theirs = prepare(info, True, near, f, s, ())

    finish = functools.partial(apply_states, info, args, partials)
    kept_heads, other_heads = ((0, 0), (1, 0)), ((0, 1), (1, 1))
    t_other = send(across, row_swap)
    t_kept = mine, send(theirs, core_swap)
    late = prepare(info, False, near, f, s, (across,))
    *outs, zero = finish(True, kept_heads, t_kept, None, (across, late[0]))
    t_rest = t_other + rest_mine + zero, send(t_other + rest_theirs, core_swap)

    across, mine, theirs = (coming + x for x in late[:3])
    u_other = send(across, row_swap)
    u_kept = mine, send(theirs, core_swap)
    *outs, _ = finish(True, other_heads, t_rest, outs, (across,))
    *outs, zero = finish(False, kept_heads, u_kept, outs)
    u_rest = u_other + late[3] + zero, send(u_other + late[4], core_swap)
    *outs, _ = finish(False, other_heads, u_rest, outs)
    return tuple(outs)


def solution(mesh):
    spec = P(("group", "seq"), None)
    return jax.shard_map(
        body, mesh=mesh, in_specs=(spec,) * 4, out_specs=(spec,) * 4, check_vma=False
    )
```

```python
import functools

import jax
import jax.numpy as jnp
from jax import lax
from jax.experimental import pallas as pl
from jax.experimental.pallas import tpu as pltpu
from jax.sharding import PartitionSpec as P

DH = 128
F32 = jnp.float32
BF16 = jnp.bfloat16
MIB = 2**20
SMALL = pl.CostEstimate(flops=1, bytes_accessed=1, transcendentals=0)

CORE, ROW, EVEN, EARLY_KV, START, INNER = range(6)

IN_SMEM = pl.BlockSpec(memory_space=pltpu.SMEM)
IN_VMEM = pl.BlockSpec(memory_space=pltpu.VMEM)
IN_HBM = pl.BlockSpec(memory_space=pltpu.HBM)


def rows_scale(start, count):
    where = start + lax.broadcasted_iota(jnp.int32, (count, DH), 0)
    return 1.0 / jnp.sqrt(DH * (where.astype(F32) + 1.0))


def dot(a, b, ca, cb):
    return lax.dot_general(a, b, (((ca,), (cb,)), ((), ())), preferred_element_type=F32)


def first_head(info, side, part, quarter):
    core = info[CORE] if side == 0 else 1 - info[CORE]
    row = info[ROW] if part == 0 else 1 - info[ROW]
    return (core * 2 + row) * quarter


def half_cols(info, side, width):
    core = info[CORE] if side == 0 else 1 - info[CORE]
    half = width // 2
    return pl.multiple_of(core * half, half)


def state_products(is_kv, side, quarter, info, q, k, v, d, out):
    count = q.shape[0]

    @pl.when(is_kv)
    def _():
        for part in range(2):
            head = first_head(info, side, part, quarter)
            for i in range(quarter):
                cols = pl.ds(pl.multiple_of((head + i) * DH, DH), DH)
                out[part * quarter + i] = dot(k[:, cols], v[:, cols], 0, 0)

    @pl.when(jnp.logical_not(is_kv))
    def _():
        scale = rows_scale(info[START], count)
        for part in range(2):
            head = first_head(info, side, part, quarter)
            for i in range(quarter):
                cols = pl.ds(pl.multiple_of((head + i) * DH, DH), DH)
                scaled = (d[:, cols].astype(F32) * scale).astype(BF16)
                out[part * quarter + i] = dot(q[:, cols], scaled, 0, 0)


def pair_copies(info, side, width, rows, sems, *pair):
    half = width // 2
    for n, (there, here) in enumerate(pair):
        for step in range(there.shape[0] // rows):
            at = pl.ds(step * rows, rows), pl.ds(half_cols(info, side, width), half)
            yield pltpu.make_async_copy(there.at[at], here.at[at], sems.at[n, step])


def first_kernel(quarter, rows, info, q, k, v, d, out, left, right, sems):
    width = q.shape[1]
    is_kv = info[EVEN] == 1

    def copies(side, a, b):
        return pair_copies(info, side, width, rows, sems.at[side], (a, left), (b, right))

    @pl.when(is_kv)
    def _():
        for side in (1, 0):
            for copy in copies(side, k, v):
                copy.start()

    @pl.when(jnp.logical_not(is_kv))
    def _():
        for side in (1, 0):
            for copy in copies(side, q, d):
                copy.start()

    for copy in copies(1, k, v):
        copy.wait()
    state_products(is_kv, 1, quarter, info, left, left, right, right, out)
    for copy in copies(0, k, v):
        copy.wait()


def first_state(info, args):
    count, width = args[0].shape
    heads = width // DH
    rows = count // 4
    return pl.pallas_call(
        functools.partial(first_kernel, heads // 4, rows),
        out_shape=[jax.ShapeDtypeStruct((heads // 2, DH, DH), F32)]
        + [jax.ShapeDtypeStruct((count, width), BF16)] * 2,
        in_specs=[IN_SMEM] + [IN_HBM] * 4,
        out_specs=[IN_VMEM] * 3,
        scratch_shapes=[pltpu.SemaphoreType.DMA((2, 2, count // rows))],
        compiler_params=pltpu.CompilerParams(vmem_limit_bytes=4 * MIB),
        cost_estimate=SMALL,
        name="first",
    )(info, *args)


def own_kernel(quarter, info, left, right, out):
    state_products(info[EVEN] == 1, 0, quarter, info, left, left, right, right, out)


def own_state(info, left, right):
    width = left.shape[1]
    heads = width // DH
    return pl.pallas_call(
        functools.partial(own_kernel, heads // 4),
        out_shape=jax.ShapeDtypeStruct((heads // 2, DH, DH), F32),
        in_specs=[IN_SMEM] + [IN_VMEM] * 2,
        out_specs=IN_VMEM,
        compiler_params=pltpu.CompilerParams(vmem_limit_bytes=4 * MIB),
        cost_estimate=SMALL,
        name="own",
    )(info, left, right)


def second_kernel(quarter, rows, n_after, info, q, k, v, d, *refs):
    sib, own, qv, kv, vv, dv, sems = refs[n_after:]
    width = q.shape[1]
    is_kv = info[EVEN] != 1

    def copies(n, side, *pair):
        return pair_copies(info, side, width, rows, sems.at[n], *pair)

    keys, queries = ((k, kv), (v, vv)), ((q, qv), (d, dv))

    def start(*pairs):
        for n, pair in enumerate(pairs):
            for copy in copies(n, 1 - n % 2, *pair):
                copy.start()

    @pl.when(is_kv)
    def _():
        start(keys, keys, queries, queries)

    @pl.when(jnp.logical_not(is_kv))
    def _():
        start(queries, queries, keys, keys)

    for n, out in ((0, sib), (1, own)):
        for copy in copies(n, 1 - n, *keys):
            copy.wait()
        state_products(is_kv, 1 - n, quarter, info, qv, kv, vv, dv, out)
    for n in (2, 3):
        for copy in copies(n, 1 - n % 2, *keys):
            copy.wait()


def second_states(info, args, after):
    count, width = args[0].shape
    heads = width // DH
    rows = count // 4
    return pl.pallas_call(
        functools.partial(second_kernel, heads // 4, rows, len(after)),
        out_shape=[jax.ShapeDtypeStruct((heads // 2, DH, DH), F32)] * 2
        + [jax.ShapeDtypeStruct((count, width), BF16)] * 4,
        in_specs=[IN_SMEM] + [IN_HBM] * 4 + [IN_VMEM] * len(after),
        out_specs=[IN_VMEM] * 6,
        scratch_shapes=[pltpu.SemaphoreType.DMA((4, 2, count // rows))],
        compiler_params=pltpu.CompilerParams(vmem_limit_bytes=4 * MIB),
        cost_estimate=SMALL,
        name="second",
    )(info, *args, *after)


def local_kernel(kinds, quarter, mark, n_after, info, q, k, v, d, *refs):
    *parts, flag = refs[n_after:]
    flag[...] = jnp.full(flag.shape, jnp.where(info[INNER] == 1, mark, 0.0), F32)
    count = q.shape[0]
    two = 2
    scale = rows_scale(info[START], count)
    lower = lax.broadcasted_iota(jnp.int32, (count, count), 1) <= lax.broadcasted_iota(
        jnp.int32, (count, count), 0
    )

    for n, (side, part) in enumerate(kinds):
        first = first_head(info, side, part, quarter)
        o_ref, dq_ref, dk_ref, dv_ref = parts[4 * n : 4 * n + 4]

        def step(g, carry):
            for i in range(two):
                to = pl.ds(pl.multiple_of((g * two + i) * DH, DH), DH)
                cols = pl.ds(pl.multiple_of((first + g * two + i) * DH, DH), DH)
                qh, kh, vh = q[:, cols], k[:, cols], v[:, cols]
                ph = (d[:, cols].astype(F32) * scale).astype(BF16)
                scores = jnp.where(lower, dot(qh, kh, 1, 1), 0.0).astype(BF16)
                back = jnp.where(lower, dot(ph, vh, 1, 1), 0.0).astype(BF16)
                o_ref[:, to] = dot(scores, vh, 1, 0)
                dq_ref[:, to] = dot(back, kh, 1, 0)
                dk_ref[:, to] = dot(back, qh, 0, 0)
                dv_ref[:, to] = dot(scores, ph, 0, 0)
            return carry

        lax.fori_loop(0, quarter // two, step, 0)


def local_part(info, args, kinds, mark, after=()):
    count, width = args[0].shape
    quarter = width // DH // 4
    *parts, flag = pl.pallas_call(
        functools.partial(local_kernel, kinds, quarter, mark, len(after)),
        out_shape=[jax.ShapeDtypeStruct((count, width // 4), F32)] * (4 * len(kinds))
        + [jax.ShapeDtypeStruct((quarter, DH, DH), F32)],
        in_specs=[IN_SMEM] + [IN_VMEM] * (4 + len(after)),
        out_specs=[IN_VMEM] * (4 * len(kinds) + 1),
        compiler_params=pltpu.CompilerParams(vmem_limit_bytes=8 * MIB),
        cost_estimate=SMALL,
        name="local",
    )(info, *args, *after)
    return {kind: parts[4 * n : 4 * n + 4] for n, kind in enumerate(kinds)}, flag


def apply_kernel(early, kinds, quarter, n_filled, n_after, info, *refs):
    q, k, v, d = refs[:4]
    refs = refs[4:]
    partials = [refs[4 * n : 4 * n + 4] for n in range(len(kinds))]
    refs = refs[4 * len(kinds) :]
    state_refs, refs = refs[: len(kinds)], refs[len(kinds) + n_filled + n_after :]
    o_hbm, dq_hbm, dk_hbm, dv_hbm, zero, one, other, sems = refs
    zero[...] = jnp.zeros_like(zero)
    count = q.shape[0]
    two = 2
    is_kv = (info[EARLY_KV] == 1) if early else (info[EARLY_KV] != 1)
    steps = [(n, j) for n in range(len(kinds)) for j in range(quarter // two)]
    starts = [first_head(info, side, part, quarter) * DH for side, part in kinds]

    def columns(n, head):
        return pl.multiple_of(starts[n] + head * DH, DH)

    def copies(step, a, b):
        n, j = steps[step]
        here = pl.ds(step * two * DH, two * DH)
        there = pl.ds(pl.multiple_of(starts[n] + j * two * DH, two * DH), two * DH)
        return (
            pltpu.make_async_copy(one.at[:, here], a.at[:, there], sems.at[step, 0]),
            pltpu.make_async_copy(other.at[:, here], b.at[:, there], sems.at[step, 1]),
        )

    def each_head(products, a, b):
        for step, (n, j) in enumerate(steps):
            for i in range(two):
                head = j * two + i
                cols = pl.ds(columns(n, head), DH)
                at = head * DH
                here = slice((step * two + i) * DH, (step * two + i + 1) * DH)
                one[:, here], other[:, here] = products(
                    cols, partials[n], slice(at, at + DH), state_refs[n][head].astype(BF16)
                )
            for copy in copies(step, a, b):
                copy.start()

    @pl.when(is_kv)
    def _():
        scale = rows_scale(info[START], count)

        def products(cols, partial, at, kv):
            o_part, dq_part = partial[0][:, at], partial[1][:, at]
            ph = (d[:, cols].astype(F32) * scale).astype(BF16)
            return (
                ((o_part + dot(q[:, cols], kv, 1, 0)) * scale).astype(BF16),
                (dq_part + dot(ph, kv, 1, 1)).astype(BF16),
            )

        each_head(products, o_hbm, dq_hbm)

    @pl.when(jnp.logical_not(is_kv))
    def _():
        def products(cols, partial, at, gr):
            dk_part, dv_part = partial[2][:, at], partial[3][:, at]
            return (
                (dk_part + dot(v[:, cols], gr, 1, 1)).astype(BF16),
                (dv_part + dot(k[:, cols], gr, 1, 0)).astype(BF16),
            )

        each_head(products, dk_hbm, dv_hbm)

    for step in range(len(steps)):
        for copy in copies(step, o_hbm, dq_hbm):
            copy.wait()


def apply_states(info, args, partials, early, kinds, arrays, outs, after=()):
    count, width = args[0].shape
    quarter = width // DH // 4
    filled = () if outs is None else tuple(outs)
    partials = [x for kind in kinds for x in partials[kind]]
    first_out = 5 + len(partials) + len(kinds)
    columns = len(kinds) * quarter * DH
    return pl.pallas_call(
        functools.partial(
            apply_kernel, early, kinds, quarter, len(filled), len(after)
        ),
        out_shape=[jax.ShapeDtypeStruct((count, width), BF16)] * 4
        + [jax.ShapeDtypeStruct((quarter, DH, DH), F32)],
        in_specs=[IN_SMEM]
        + [IN_VMEM] * (4 + len(partials) + len(kinds))
        + [IN_HBM] * len(filled)
        + [IN_VMEM] * len(after),
        out_specs=[IN_HBM] * 4 + [IN_VMEM],
        scratch_shapes=[
            pltpu.VMEM((count, columns), BF16),
            pltpu.VMEM((count, columns), BF16),
            pltpu.SemaphoreType.DMA((columns // (2 * DH), 2)),
        ],
        input_output_aliases={first_out + n: n for n in range(len(filled))},
        compiler_params=pltpu.CompilerParams(vmem_limit_bytes=8 * MIB),
        cost_estimate=SMALL,
        name="apply",
    )(info, *args, *partials, *arrays, *filled, *after)


def prepare_kernel(early, n_after, info, *refs):
    near, f_own, f_got, f_keep, f_other, s_own, s_got, s_keep, s_other = refs[:9]
    across, mine, theirs, rest_mine, rest_theirs = refs[9 + n_after :]
    quarter = near.shape[0]
    is_kv = (info[EARLY_KV] == 1) if early else (info[EARLY_KV] != 1)
    is_first = (info[EVEN] == 1) == is_kv
    takes_near = (info[INNER] == 1) if early else (info[INNER] != 1)
    after_row = is_kv == (info[ROW] == 1)
    after_core = is_kv == (info[CORE] == 1)
    for i in range(quarter):
        val = jnp.where(takes_near, near[i], 0.0)
        keep = jnp.where(is_first, f_keep[i], s_keep[i])
        other = jnp.where(is_first, f_other[i], s_other[i])
        own = jnp.where(is_first, f_own[i], s_own[i])
        got = jnp.where(is_first, f_got[i], s_got[i])
        across[i] = val + jnp.where(after_row, 0.0, keep)
        here = val + jnp.where(after_row, other, 0.0)
        mine[i] = here + jnp.where(after_core, got, 0.0)
        theirs[i] = here + jnp.where(after_core, 0.0, own)
        own = jnp.where(is_first, f_own[quarter + i], s_own[quarter + i])
        got = jnp.where(is_first, f_got[quarter + i], s_got[quarter + i])
        rest_mine[i] = jnp.where(after_core, got, 0.0)
        rest_theirs[i] = jnp.where(after_core, 0.0, own)


def prepare(info, early, near, f, s, after):
    return pl.pallas_call(
        functools.partial(prepare_kernel, early, len(after)),
        out_shape=[jax.ShapeDtypeStruct(near.shape, F32)] * 5,
        in_specs=[IN_SMEM] + [IN_VMEM] * (9 + len(after)),
        out_specs=[IN_VMEM] * 5,
        compiler_params=pltpu.CompilerParams(vmem_limit_bytes=4 * MIB),
        cost_estimate=SMALL,
        name="prepare",
    )(info, near, *f, *s, *after)


def send(array, pairs):
    return lax.ppermute(array, "seq", pairs)


def plane_scan(planes, kv, qg):
    def scan(x, sign):
        def shift(x, by):
            pairs = [(a, a + sign * by) for a in range(planes) if 0 <= a + sign * by < planes]
            return send(x, spread_pairs(pairs))

        x, by = shift(x, 1), 1
        while by < planes:
            x, by = x + shift(x, by), 2 * by
        return x

    return scan(kv, 1), scan(qg, -1)


def spread_pairs(pairs):
    return [(4 * a + i, 4 * b + i) for a, b in pairs for i in range(4)]


def body(query, key_in, value, d_out):
    args = (query, key_in, value, d_out)
    count, width = query.shape
    heads = width // DH
    size, place = lax.axis_size("seq"), lax.axis_index("seq")
    planes = size // 4
    core, row, plane = place % 2, (place // 2) % 2, place // 4
    even = plane % 2 == 0
    early_kv = plane < planes // 2
    inner = (plane == 1) | (plane == 2) | (planes != 4)
    info = jnp.stack([core, row, even, early_kv, place * count, inner]).astype(jnp.int32)
    core_swap = [(i, i ^ 1) for i in range(size)]
    row_swap = [(i, i ^ 2) for i in range(size)]
    far_args = tuple(pltpu.with_memory_space_constraint(x, pltpu.HBM) for x in args)

    quarter = heads // 4

    def halves(own, got):
        return own[:quarter] + got[:quarter], own[quarter:] + got[quarter:]

    kinds = (0, 0), (0, 1), (1, 0), (1, 1)
    f_sib, left, right = first_state(info, far_args)
    f_got = send(f_sib, core_swap)
    f_own = own_state(info, left, right)
    f_keep, f_give = halves(f_own, f_got)
    f_other = send(f_give, row_swap)
    s_sib, s_own, *args = second_states(info, far_args, (f_give,))
    part_a, zero = local_part(info, args, kinds[:1], 0.0, (s_own,))
    s_got = send(s_sib, core_swap)
    s_keep, s_give = halves(s_own, s_got)
    s_other = send(s_give, row_swap)
    f_total = f_keep + f_other + zero
    f = f_own, f_got, f_keep, f_other
    s = s_own, s_got, s_keep, s_other
    part_b, inside = local_part(info, args, kinds[1:], 1.0, (s_give,))
    partials = part_a | part_b
    if planes == 4:
        near = send(f_total, spread_pairs([(0, 1), (1, 0), (2, 3), (3, 2)]))
        pair = jnp.where(inside > 0.0, s_keep + s_other + near, 0.0)
        middle = send(pair, spread_pairs([(1, 2), (2, 1)]) + core_swap[:4] + core_swap[-4:])
        outer = send(middle, spread_pairs([(0, 1), (1, 0), (2, 3), (3, 2)]))
        coming = middle + outer
    else:
        s_total = s_keep + s_other
        kv, qg = plane_scan(
            planes, jnp.where(even, f_total, s_total), jnp.where(even, s_total, f_total)
        )
        near = pair = jnp.where(early_kv, kv, qg)
        coming = jnp.where(early_kv, qg, kv)
    across, mine, theirs, rest_mine, rest_theirs = prepare(info, True, near, f, s, ())

    finish = functools.partial(apply_states, info, args, partials)
    kept_heads, other_heads = kinds[0::2], kinds[1::2]
    t_other = send(across, row_swap)
    t_kept = mine, send(theirs, core_swap)
    late = prepare(info, False, near, f, s, (across,))
    *outs, zero = finish(True, kept_heads, t_kept, None, (across, late[0]))
    t_rest = t_other + rest_mine + zero, send(t_other + rest_theirs, core_swap)

    across, mine, theirs = (coming + x for x in late[:3])
    u_other = send(across, row_swap)
    u_kept = mine, send(theirs, core_swap)
    *outs, _ = finish(True, other_heads, t_rest, outs, (across,))
    *outs, zero = finish(False, kept_heads, u_kept, outs)
    u_rest = u_other + late[3] + zero, send(u_other + late[4], core_swap)
    *outs, _ = finish(False, other_heads, u_rest, outs)
    return tuple(outs)


def solution(mesh):
    spec = P(("group", "seq"), None)
    return jax.shard_map(
        body, mesh=mesh, in_specs=(spec,) * 4, out_specs=(spec,) * 4, check_vma=False
    )
```

```python
import functools

import jax
import jax.numpy as jnp
from jax import lax
from jax.experimental import pallas as pl
from jax.experimental.pallas import tpu as pltpu
from jax.sharding import PartitionSpec as P

DH = 128
F32 = jnp.float32
BF16 = jnp.bfloat16
MIB = 2**20
SMALL = pl.CostEstimate(flops=1, bytes_accessed=1, transcendentals=0)

CORE, ROW, EVEN, EARLY_KV, START, INNER = range(6)

IN_SMEM = pl.BlockSpec(memory_space=pltpu.SMEM)
IN_VMEM = pl.BlockSpec(memory_space=pltpu.VMEM)
IN_HBM = pl.BlockSpec(memory_space=pltpu.HBM)


def rows_scale(start, count):
    where = start + lax.broadcasted_iota(jnp.int32, (count, DH), 0)
    return 1.0 / jnp.sqrt(DH * (where.astype(F32) + 1.0))


def dot(a, b, ca, cb):
    return lax.dot_general(a, b, (((ca,), (cb,)), ((), ())), preferred_element_type=F32)


def first_head(info, side, part, quarter):
    core = info[CORE] if side == 0 else 1 - info[CORE]
    row = info[ROW] if part == 0 else 1 - info[ROW]
    return (core * 2 + row) * quarter


def half_cols(info, side, width):
    core = info[CORE] if side == 0 else 1 - info[CORE]
    half = width // 2
    return pl.multiple_of(core * half, half)


def state_products(is_kv, side, quarter, info, q, k, v, d, out):
    count = q.shape[0]

    @pl.when(is_kv)
    def _():
        for part in range(2):
            head = first_head(info, side, part, quarter)
            for i in range(quarter):
                cols = pl.ds(pl.multiple_of((head + i) * DH, DH), DH)
                out[part * quarter + i] = dot(k[:, cols], v[:, cols], 0, 0)

    @pl.when(jnp.logical_not(is_kv))
    def _():
        scale = rows_scale(info[START], count)
        for part in range(2):
            head = first_head(info, side, part, quarter)
            for i in range(quarter):
                cols = pl.ds(pl.multiple_of((head + i) * DH, DH), DH)
                scaled = (d[:, cols].astype(F32) * scale).astype(BF16)
                out[part * quarter + i] = dot(q[:, cols], scaled, 0, 0)


def pair_copies(info, side, width, rows, sems, *pair):
    half = width // 2
    for n, (there, here) in enumerate(pair):
        for step in range(there.shape[0] // rows):
            at = pl.ds(step * rows, rows), pl.ds(half_cols(info, side, width), half)
            yield pltpu.make_async_copy(there.at[at], here.at[at], sems.at[n, step])


def first_kernel(quarter, rows, info, q, k, v, d, out, left, right, sems):
    width = q.shape[1]
    is_kv = info[EVEN] == 1

    def copies(side, a, b):
        return pair_copies(info, side, width, rows, sems.at[side], (a, left), (b, right))

    @pl.when(is_kv)
    def _():
        for side in (1, 0):
            for copy in copies(side, k, v):
                copy.start()

    @pl.when(jnp.logical_not(is_kv))
    def _():
        for side in (1, 0):
            for copy in copies(side, q, d):
                copy.start()

    for copy in copies(1, k, v):
        copy.wait()
    state_products(is_kv, 1, quarter, info, left, left, right, right, out)
    for copy in copies(0, k, v):
        copy.wait()


def first_state(info, args):
    count, width = args[0].shape
    heads = width // DH
    rows = count // 4
    return pl.pallas_call(
        functools.partial(first_kernel, heads // 4, rows),
        out_shape=[jax.ShapeDtypeStruct((heads // 2, DH, DH), F32)]
        + [jax.ShapeDtypeStruct((count, width), BF16)] * 2,
        in_specs=[IN_SMEM] + [IN_HBM] * 4,
        out_specs=[IN_VMEM] * 3,
        scratch_shapes=[pltpu.SemaphoreType.DMA((2, 2, count // rows))],
        compiler_params=pltpu.CompilerParams(vmem_limit_bytes=4 * MIB),
        cost_estimate=SMALL,
        name="first",
    )(info, *args)


def own_kernel(quarter, info, left, right, out):
    state_products(info[EVEN] == 1, 0, quarter, info, left, left, right, right, out)


def own_state(info, left, right):
    width = left.shape[1]
    heads = width // DH
    return pl.pallas_call(
        functools.partial(own_kernel, heads // 4),
        out_shape=jax.ShapeDtypeStruct((heads // 2, DH, DH), F32),
        in_specs=[IN_SMEM] + [IN_VMEM] * 2,
        out_specs=IN_VMEM,
        compiler_params=pltpu.CompilerParams(vmem_limit_bytes=4 * MIB),
        cost_estimate=SMALL,
        name="own",
    )(info, left, right)


def second_kernel(quarter, rows, n_after, info, q, k, v, d, *refs):
    sib, own, qv, kv, vv, dv, sems = refs[n_after:]
    width = q.shape[1]
    is_kv = info[EVEN] != 1

    def copies(n, side, *pair):
        return pair_copies(info, side, width, rows, sems.at[n], *pair)

    keys, queries = ((k, kv), (v, vv)), ((q, qv), (d, dv))

    def start(*pairs):
        for n, pair in enumerate(pairs):
            for copy in copies(n, 1 - n % 2, *pair):
                copy.start()

    @pl.when(is_kv)
    def _():
        start(keys, keys, queries, queries)

    @pl.when(jnp.logical_not(is_kv))
    def _():
        start(queries, queries, keys, keys)

    for n, out in ((0, sib), (1, own)):
        for copy in copies(n, 1 - n, *keys):
            copy.wait()
        state_products(is_kv, 1 - n, quarter, info, qv, kv, vv, dv, out)
    for n in (2, 3):
        for copy in copies(n, 1 - n % 2, *keys):
            copy.wait()


def second_states(info, args, after):
    count, width = args[0].shape
    heads = width // DH
    rows = count // 4
    return pl.pallas_call(
        functools.partial(second_kernel, heads // 4, rows, len(after)),
        out_shape=[jax.ShapeDtypeStruct((heads // 2, DH, DH), F32)] * 2
        + [jax.ShapeDtypeStruct((count, width), BF16)] * 4,
        in_specs=[IN_SMEM] + [IN_HBM] * 4 + [IN_VMEM] * len(after),
        out_specs=[IN_VMEM] * 6,
        scratch_shapes=[pltpu.SemaphoreType.DMA((4, 2, count // rows))],
        compiler_params=pltpu.CompilerParams(vmem_limit_bytes=4 * MIB),
        cost_estimate=SMALL,
        name="second",
    )(info, *args, *after)


def local_kernel(kinds, quarter, mark, n_after, info, q, k, v, d, *refs):
    *parts, flag = refs[n_after:]
    flag[...] = jnp.full(flag.shape, jnp.where(info[INNER] == 1, mark, 0.0), F32)
    count = q.shape[0]
    two = 2
    scale = rows_scale(info[START], count)
    lower = lax.broadcasted_iota(jnp.int32, (count, count), 1) <= lax.broadcasted_iota(
        jnp.int32, (count, count), 0
    )

    for n, (side, part) in enumerate(kinds):
        first = first_head(info, side, part, quarter)
        o_ref, dq_ref, dk_ref, dv_ref = parts[4 * n : 4 * n + 4]

        def step(g, carry):
            for i in range(two):
                to = pl.ds(pl.multiple_of((g * two + i) * DH, DH), DH)
                cols = pl.ds(pl.multiple_of((first + g * two + i) * DH, DH), DH)
                qh, kh, vh = q[:, cols], k[:, cols], v[:, cols]
                ph = (d[:, cols].astype(F32) * scale).astype(BF16)
                scores = jnp.where(lower, dot(qh, kh, 1, 1), 0.0).astype(BF16)
                back = jnp.where(lower, dot(ph, vh, 1, 1), 0.0).astype(BF16)
                o_ref[:, to] = dot(scores, vh, 1, 0)
                dq_ref[:, to] = dot(back, kh, 1, 0)
                dk_ref[:, to] = dot(back, qh, 0, 0)
                dv_ref[:, to] = dot(scores, ph, 0, 0)
            return carry

        lax.fori_loop(0, quarter // two, step, 0)


def local_part(info, args, kinds, mark, after=()):
    count, width = args[0].shape
    quarter = width // DH // 4
    *parts, flag = pl.pallas_call(
        functools.partial(local_kernel, kinds, quarter, mark, len(after)),
        out_shape=[jax.ShapeDtypeStruct((count, width // 4), F32)] * (4 * len(kinds))
        + [jax.ShapeDtypeStruct((quarter, DH, DH), F32)],
        in_specs=[IN_SMEM] + [IN_VMEM] * (4 + len(after)),
        out_specs=[IN_VMEM] * (4 * len(kinds) + 1),
        compiler_params=pltpu.CompilerParams(vmem_limit_bytes=8 * MIB),
        cost_estimate=SMALL,
        name="local",
    )(info, *args, *after)
    return {kind: parts[4 * n : 4 * n + 4] for n, kind in enumerate(kinds)}, flag


def apply_kernel(early, kinds, pieces, quarter, n_filled, n_after, info, *refs):
    q, k, v, d = refs[:4]
    refs = refs[4:]
    partials = [refs[4 * n : 4 * n + 4] for n in range(len(kinds))]
    refs = refs[4 * len(kinds) :]
    n_states = len(kinds) * pieces
    state_refs, refs = refs[:n_states], refs[n_states + n_filled + n_after :]
    each = quarter // pieces
    o_hbm, dq_hbm, dk_hbm, dv_hbm, zero, one, other, sems = refs
    zero[...] = jnp.zeros_like(zero)
    count = q.shape[0]
    two = 2
    is_kv = (info[EARLY_KV] == 1) if early else (info[EARLY_KV] != 1)
    steps = [(n, j) for n in range(len(kinds)) for j in range(quarter // two)]
    starts = [first_head(info, side, part, quarter) * DH for side, part in kinds]

    def columns(n, head):
        return pl.multiple_of(starts[n] + head * DH, DH)

    def copies(step, a, b):
        n, j = steps[step]
        here = pl.ds(step * two * DH, two * DH)
        there = pl.ds(pl.multiple_of(starts[n] + j * two * DH, two * DH), two * DH)
        return (
            pltpu.make_async_copy(one.at[:, here], a.at[:, there], sems.at[step, 0]),
            pltpu.make_async_copy(other.at[:, here], b.at[:, there], sems.at[step, 1]),
        )

    def each_head(products, a, b):
        for step, (n, j) in enumerate(steps):
            for i in range(two):
                head = j * two + i
                cols = pl.ds(columns(n, head), DH)
                at = head * DH
                here = slice((step * two + i) * DH, (step * two + i + 1) * DH)
                one[:, here], other[:, here] = products(
                    cols, partials[n], slice(at, at + DH), state_refs[n * pieces + head // each][head % each].astype(BF16)
                )
            for copy in copies(step, a, b):
                copy.start()

    @pl.when(is_kv)
    def _():
        scale = rows_scale(info[START], count)

        def products(cols, partial, at, kv):
            o_part, dq_part = partial[0][:, at], partial[1][:, at]
            ph = (d[:, cols].astype(F32) * scale).astype(BF16)
            return (
                ((o_part + dot(q[:, cols], kv, 1, 0)) * scale).astype(BF16),
                (dq_part + dot(ph, kv, 1, 1)).astype(BF16),
            )

        each_head(products, o_hbm, dq_hbm)

    @pl.when(jnp.logical_not(is_kv))
    def _():
        def products(cols, partial, at, gr):
            dk_part, dv_part = partial[2][:, at], partial[3][:, at]
            return (
                (dk_part + dot(v[:, cols], gr, 1, 1)).astype(BF16),
                (dv_part + dot(k[:, cols], gr, 1, 0)).astype(BF16),
            )

        each_head(products, dk_hbm, dv_hbm)

    for step in range(len(steps)):
        for copy in copies(step, o_hbm, dq_hbm):
            copy.wait()


def apply_states(info, args, partials, early, kinds, arrays, outs, after=()):
    count, width = args[0].shape
    quarter = width // DH // 4
    filled = () if outs is None else tuple(outs)
    partials = [x for kind in kinds for x in partials[kind]]
    first_out = 5 + len(partials) + len(arrays)
    columns = len(kinds) * quarter * DH
    return pl.pallas_call(
        functools.partial(
            apply_kernel, early, kinds, len(arrays) // len(kinds), quarter, len(filled), len(after)
        ),
        out_shape=[jax.ShapeDtypeStruct((count, width), BF16)] * 4
        + [jax.ShapeDtypeStruct((quarter, DH, DH), F32)],
        in_specs=[IN_SMEM]
        + [IN_VMEM] * (4 + len(partials) + len(arrays))
        + [IN_HBM] * len(filled)
        + [IN_VMEM] * len(after),
        out_specs=[IN_HBM] * 4 + [IN_VMEM],
        scratch_shapes=[
            pltpu.VMEM((count, columns), BF16),
            pltpu.VMEM((count, columns), BF16),
            pltpu.SemaphoreType.DMA((columns // (2 * DH), 2)),
        ],
        input_output_aliases={first_out + n: n for n in range(len(filled))},
        compiler_params=pltpu.CompilerParams(vmem_limit_bytes=8 * MIB),
        cost_estimate=SMALL,
        name="apply",
    )(info, *args, *partials, *arrays, *filled, *after)


def prepare_kernel(early, n_after, info, *refs):
    near, f_own, f_got, f_keep, f_other, s_own, s_got, s_keep, s_other = refs[:9]
    across, mine, theirs, rest_mine, rest_theirs = refs[9 + n_after :]
    quarter = near.shape[0]
    is_kv = (info[EARLY_KV] == 1) if early else (info[EARLY_KV] != 1)
    is_first = (info[EVEN] == 1) == is_kv
    takes_near = (info[INNER] == 1) if early else (info[INNER] != 1)
    after_row = is_kv == (info[ROW] == 1)
    after_core = is_kv == (info[CORE] == 1)
    for i in range(quarter):
        val = jnp.where(takes_near, near[i], 0.0)
        keep = jnp.where(is_first, f_keep[i], s_keep[i])
        other = jnp.where(is_first, f_other[i], s_other[i])
        own = jnp.where(is_first, f_own[i], s_own[i])
        got = jnp.where(is_first, f_got[i], s_got[i])
        across[i] = val + jnp.where(after_row, 0.0, keep)
        here = val + jnp.where(after_row, other, 0.0)
        mine[i] = here + jnp.where(after_core, got, 0.0)
        theirs[i] = here + jnp.where(after_core, 0.0, own)
        own = jnp.where(is_first, f_own[quarter + i], s_own[quarter + i])
        got = jnp.where(is_first, f_got[quarter + i], s_got[quarter + i])
        rest_mine[i] = jnp.where(after_core, got, 0.0)
        rest_theirs[i] = jnp.where(after_core, 0.0, own)


def prepare(info, early, near, f, s, after):
    return pl.pallas_call(
        functools.partial(prepare_kernel, early, len(after)),
        out_shape=[jax.ShapeDtypeStruct(near.shape, F32)] * 5,
        in_specs=[IN_SMEM] + [IN_VMEM] * (9 + len(after)),
        out_specs=[IN_VMEM] * 5,
        compiler_params=pltpu.CompilerParams(vmem_limit_bytes=4 * MIB),
        cost_estimate=SMALL,
        name="prepare",
    )(info, near, *f, *s, *after)


def send(array, pairs):
    return lax.ppermute(array, "seq", pairs)


def plane_scan(planes, kv, qg):
    def scan(x, sign):
        def shift(x, by):
            pairs = [(a, a + sign * by) for a in range(planes) if 0 <= a + sign * by < planes]
            return send(x, spread_pairs(pairs))

        x, by = shift(x, 1), 1
        while by < planes:
            x, by = x + shift(x, by), 2 * by
        return x

    return scan(kv, 1), scan(qg, -1)


def spread_pairs(pairs):
    return [(4 * a + i, 4 * b + i) for a, b in pairs for i in range(4)]


def body(query, key_in, value, d_out):
    args = (query, key_in, value, d_out)
    count, width = query.shape
    heads = width // DH
    size, place = lax.axis_size("seq"), lax.axis_index("seq")
    planes = size // 4
    core, row, plane = place % 2, (place // 2) % 2, place // 4
    even = plane % 2 == 0
    early_kv = plane < planes // 2
    inner = (plane == 1) | (plane == 2) | (planes != 4)
    info = jnp.stack([core, row, even, early_kv, place * count, inner]).astype(jnp.int32)
    core_swap = [(i, i ^ 1) for i in range(size)]
    row_swap = [(i, i ^ 2) for i in range(size)]
    far_args = tuple(pltpu.with_memory_space_constraint(x, pltpu.HBM) for x in args)

    quarter = heads // 4
    cuts = slice(0, quarter // 2), slice(quarter // 2, quarter)

    def halves(own, got):
        return own[:quarter] + got[:quarter], own[quarter:] + got[quarter:]

    kinds = (0, 0), (0, 1), (1, 0), (1, 1)
    f_sib, left, right = first_state(info, far_args)
    f_got = send(f_sib, core_swap)
    f_own = own_state(info, left, right)
    f_keep, f_give = halves(f_own, f_got)
    f_other = send(f_give, row_swap)
    s_sib, s_own, *args = second_states(info, far_args, (f_give,))
    part_a, zero = local_part(info, args, kinds[:1], 0.0, (s_own,))
    s_got = send(s_sib, core_swap)
    s_keep, s_give = halves(s_own, s_got)
    f_total = f_keep + f_other + zero
    s_give, f_total = lax.optimization_barrier((s_give, f_total))
    s_other = send(s_give, row_swap)
    f = f_own, f_got, f_keep, f_other
    s = s_own, s_got, s_keep, s_other
    part_b, inside = local_part(info, args, kinds[1:], 1.0, (s_give,))
    partials = part_a | part_b
    if planes == 4:
        near = send(f_total, spread_pairs([(0, 1), (1, 0), (2, 3), (3, 2)]))
        pair = jnp.where(inside > 0.0, s_keep + s_other + near, 0.0)
        middle = send(pair, spread_pairs([(1, 2), (2, 1)]) + core_swap[:4] + core_swap[-4:])
        outer = send(middle, spread_pairs([(0, 1), (1, 0), (2, 3), (3, 2)]))
        coming = middle + outer
    else:
        s_total = s_keep + s_other
        kv, qg = plane_scan(
            planes, jnp.where(even, f_total, s_total), jnp.where(even, s_total, f_total)
        )
        near = pair = jnp.where(early_kv, kv, qg)
        coming = jnp.where(early_kv, qg, kv)
    across, mine, theirs, rest_mine, rest_theirs = prepare(info, True, near, f, s, ())

    finish = functools.partial(apply_states, info, args, partials)
    kept_heads, other_heads = kinds[0::2], kinds[1::2]
    t_other = send(across, row_swap)
    t_kept = mine, send(theirs, core_swap)
    late = prepare(info, False, near, f, s, (across,))
    *outs, zero = finish(True, kept_heads, t_kept, None, (across, late[0]))
    t_rest = t_other + rest_mine + zero, send(t_other + rest_theirs, core_swap)

    across = coming + late[0]
    u_other = send(across, row_swap)
    u_kept = [coming[cut] + late[1][cut] for cut in cuts]
    u_kept += [send(coming[cut] + late[2][cut], core_swap) for cut in cuts]
    *outs, _ = finish(True, other_heads, t_rest, outs, (across,))
    *outs, zero = finish(False, kept_heads, u_kept, outs)
    u_rest = u_other + late[3] + zero, send(u_other + late[4], core_swap)
    *outs, _ = finish(False, other_heads, u_rest, outs)
    return tuple(outs)


def solution(mesh):
    spec = P(("group", "seq"), None)
    return jax.shard_map(
        body, mesh=mesh, in_specs=(spec,) * 4, out_specs=(spec,) * 4, check_vma=False
    )
```

```python
import functools

import jax
import jax.numpy as jnp
from jax import lax
from jax.experimental import pallas as pl
from jax.experimental.pallas import tpu as pltpu
from jax.sharding import PartitionSpec as P

DH = 128
F32 = jnp.float32
BF16 = jnp.bfloat16
MIB = 2**20
SMALL = pl.CostEstimate(flops=1, bytes_accessed=1, transcendentals=0)

CORE, ROW, EVEN, EARLY_KV, START, INNER = range(6)

IN_SMEM = pl.BlockSpec(memory_space=pltpu.SMEM)
IN_VMEM = pl.BlockSpec(memory_space=pltpu.VMEM)
IN_HBM = pl.BlockSpec(memory_space=pltpu.HBM)


def rows_scale(start, count):
    where = start + lax.broadcasted_iota(jnp.int32, (count, DH), 0)
    return 1.0 / jnp.sqrt(DH * (where.astype(F32) + 1.0))


def dot(a, b, ca, cb):
    return lax.dot_general(a, b, (((ca,), (cb,)), ((), ())), preferred_element_type=F32)


def first_head(info, side, part, quarter):
    core = info[CORE] if side == 0 else 1 - info[CORE]
    row = info[ROW] if part == 0 else 1 - info[ROW]
    return (core * 2 + row) * quarter


def half_cols(info, side, width):
    core = info[CORE] if side == 0 else 1 - info[CORE]
    half = width // 2
    return pl.multiple_of(core * half, half)


def state_products(is_kv, side, quarter, info, q, k, v, d, out):
    count = q.shape[0]
    pieces = out if isinstance(out, tuple) else (out,)
    each = pieces[0].shape[0]

    def at(n):
        return pieces[n // each].at[n % each]

    @pl.when(is_kv)
    def _():
        for part in range(2):
            head = first_head(info, side, part, quarter)
            for i in range(quarter):
                cols = pl.ds(pl.multiple_of((head + i) * DH, DH), DH)
                at(part * quarter + i)[...] = dot(k[:, cols], v[:, cols], 0, 0)

    @pl.when(jnp.logical_not(is_kv))
    def _():
        scale = rows_scale(info[START], count)
        for part in range(2):
            head = first_head(info, side, part, quarter)
            for i in range(quarter):
                cols = pl.ds(pl.multiple_of((head + i) * DH, DH), DH)
                scaled = (d[:, cols].astype(F32) * scale).astype(BF16)
                at(part * quarter + i)[...] = dot(q[:, cols], scaled, 0, 0)


def pair_copies(info, side, width, rows, sems, *pair):
    half = width // 2
    for n, (there, here) in enumerate(pair):
        for step in range(there.shape[0] // rows):
            at = pl.ds(step * rows, rows), pl.ds(half_cols(info, side, width), half)
            yield pltpu.make_async_copy(there.at[at], here.at[at], sems.at[n, step])


def first_kernel(quarter, rows, info, q, k, v, d, keep, give, left, right, sems):
    width = q.shape[1]
    is_kv = info[EVEN] == 1

    def copies(side, a, b):
        return pair_copies(info, side, width, rows, sems.at[side], (a, left), (b, right))

    @pl.when(is_kv)
    def _():
        for side in (1, 0):
            for copy in copies(side, k, v):
                copy.start()

    @pl.when(jnp.logical_not(is_kv))
    def _():
        for side in (1, 0):
            for copy in copies(side, q, d):
                copy.start()

    for copy in copies(1, k, v):
        copy.wait()
    state_products(is_kv, 1, quarter, info, left, left, right, right, (keep, give))
    for copy in copies(0, k, v):
        copy.wait()


def first_state(info, args):
    count, width = args[0].shape
    heads = width // DH
    rows = count // 4
    return pl.pallas_call(
        functools.partial(first_kernel, heads // 4, rows),
        out_shape=[jax.ShapeDtypeStruct((heads // 4, DH, DH), F32)] * 2
        + [jax.ShapeDtypeStruct((count, width), BF16)] * 2,
        in_specs=[IN_SMEM] + [IN_HBM] * 4,
        out_specs=[IN_VMEM] * 4,
        scratch_shapes=[pltpu.SemaphoreType.DMA((2, 2, count // rows))],
        compiler_params=pltpu.CompilerParams(vmem_limit_bytes=4 * MIB),
        cost_estimate=SMALL,
        name="first",
    )(info, *args)


def own_kernel(quarter, info, left, right, out):
    state_products(info[EVEN] == 1, 0, quarter, info, left, left, right, right, out)


def own_state(info, left, right):
    width = left.shape[1]
    heads = width // DH
    return pl.pallas_call(
        functools.partial(own_kernel, heads // 4),
        out_shape=jax.ShapeDtypeStruct((heads // 2, DH, DH), F32),
        in_specs=[IN_SMEM] + [IN_VMEM] * 2,
        out_specs=IN_VMEM,
        compiler_params=pltpu.CompilerParams(vmem_limit_bytes=4 * MIB),
        cost_estimate=SMALL,
        name="own",
    )(info, left, right)


def second_kernel(quarter, rows, n_after, info, q, k, v, d, *refs):
    sib, own, qv, kv, vv, dv, sems = refs[n_after:]
    width = q.shape[1]
    is_kv = info[EVEN] != 1

    def copies(n, side, *pair):
        return pair_copies(info, side, width, rows, sems.at[n], *pair)

    keys, queries = ((k, kv), (v, vv)), ((q, qv), (d, dv))

    def start(*pairs):
        for n, pair in enumerate(pairs):
            for copy in copies(n, 1 - n % 2, *pair):
                copy.start()

    @pl.when(is_kv)
    def _():
        start(keys, keys, queries, queries)

    @pl.when(jnp.logical_not(is_kv))
    def _():
        start(queries, queries, keys, keys)

    for n, out in ((0, sib), (1, own)):
        for copy in copies(n, 1 - n, *keys):
            copy.wait()
        state_products(is_kv, 1 - n, quarter, info, qv, kv, vv, dv, out)
    for n in (2, 3):
        for copy in copies(n, 1 - n % 2, *keys):
            copy.wait()


def second_states(info, args, after):
    count, width = args[0].shape
    heads = width // DH
    rows = count // 4
    return pl.pallas_call(
        functools.partial(second_kernel, heads // 4, rows, len(after)),
        out_shape=[jax.ShapeDtypeStruct((heads // 2, DH, DH), F32)] * 2
        + [jax.ShapeDtypeStruct((count, width), BF16)] * 4,
        in_specs=[IN_SMEM] + [IN_HBM] * 4 + [IN_VMEM] * len(after),
        out_specs=[IN_VMEM] * 6,
        scratch_shapes=[pltpu.SemaphoreType.DMA((4, 2, count // rows))],
        compiler_params=pltpu.CompilerParams(vmem_limit_bytes=4 * MIB),
        cost_estimate=SMALL,
        name="second",
    )(info, *args, *after)


def local_kernel(kinds, quarter, mark, n_after, info, q, k, v, d, *refs):
    *parts, flag = refs[n_after:]
    flag[...] = jnp.full(flag.shape, jnp.where(info[INNER] == 1, mark, 0.0), F32)
    count = q.shape[0]
    two = 2
    scale = rows_scale(info[START], count)
    lower = lax.broadcasted_iota(jnp.int32, (count, count), 1) <= lax.broadcasted_iota(
        jnp.int32, (count, count), 0
    )

    for n, (side, part) in enumerate(kinds):
        first = first_head(info, side, part, quarter)
        o_ref, dq_ref, dk_ref, dv_ref = parts[4 * n : 4 * n + 4]

        def step(g, carry):
            for i in range(two):
                to = pl.ds(pl.multiple_of((g * two + i) * DH, DH), DH)
                cols = pl.ds(pl.multiple_of((first + g * two + i) * DH, DH), DH)
                qh, kh, vh = q[:, cols], k[:, cols], v[:, cols]
                ph = (d[:, cols].astype(F32) * scale).astype(BF16)
                scores = jnp.where(lower, dot(qh, kh, 1, 1), 0.0).astype(BF16)
                back = jnp.where(lower, dot(ph, vh, 1, 1), 0.0).astype(BF16)
                o_ref[:, to] = dot(scores, vh, 1, 0)
                dq_ref[:, to] = dot(back, kh, 1, 0)
                dk_ref[:, to] = dot(back, qh, 0, 0)
                dv_ref[:, to] = dot(scores, ph, 0, 0)
            return carry

        lax.fori_loop(0, quarter // two, step, 0)


def local_part(info, args, kinds, mark, after=()):
    count, width = args[0].shape
    quarter = width // DH // 4
    *parts, flag = pl.pallas_call(
        functools.partial(local_kernel, kinds, quarter, mark, len(after)),
        out_shape=[jax.ShapeDtypeStruct((count, width // 4), F32)] * (4 * len(kinds))
        + [jax.ShapeDtypeStruct((quarter, DH, DH), F32)],
        in_specs=[IN_SMEM] + [IN_VMEM] * (4 + len(after)),
        out_specs=[IN_VMEM] * (4 * len(kinds) + 1),
        compiler_params=pltpu.CompilerParams(vmem_limit_bytes=8 * MIB),
        cost_estimate=SMALL,
        name="local",
    )(info, *args, *after)
    return {kind: parts[4 * n : 4 * n + 4] for n, kind in enumerate(kinds)}, flag


def apply_kernel(early, kinds, pieces, quarter, n_filled, n_after, info, *refs):
    q, k, v, d = refs[:4]
    refs = refs[4:]
    partials = [refs[4 * n : 4 * n + 4] for n in range(len(kinds))]
    refs = refs[4 * len(kinds) :]
    n_states = len(kinds) * pieces
    state_refs, refs = refs[:n_states], refs[n_states + n_filled + n_after :]
    each = quarter // pieces
    o_hbm, dq_hbm, dk_hbm, dv_hbm, zero, one, other, sems = refs
    zero[...] = jnp.zeros_like(zero)
    count = q.shape[0]
    two = 4
    is_kv = (info[EARLY_KV] == 1) if early else (info[EARLY_KV] != 1)
    steps = [(n, j) for n in range(len(kinds)) for j in range(quarter // two)]
    starts = [first_head(info, side, part, quarter) * DH for side, part in kinds]

    def columns(n, head):
        return pl.multiple_of(starts[n] + head * DH, DH)

    def copies(step, a, b):
        n, j = steps[step]
        here = pl.ds(step * two * DH, two * DH)
        there = pl.ds(pl.multiple_of(starts[n] + j * two * DH, two * DH), two * DH)
        return (
            pltpu.make_async_copy(one.at[:, here], a.at[:, there], sems.at[step, 0]),
            pltpu.make_async_copy(other.at[:, here], b.at[:, there], sems.at[step, 1]),
        )

    def each_head(products, a, b):
        for step, (n, j) in enumerate(steps):
            for i in range(two):
                head = j * two + i
                cols = pl.ds(columns(n, head), DH)
                at = head * DH
                here = slice((step * two + i) * DH, (step * two + i + 1) * DH)
                one[:, here], other[:, here] = products(
                    cols, partials[n], slice(at, at + DH), state_refs[n * pieces + head // each][head % each].astype(BF16)
                )
            for copy in copies(step, a, b):
                copy.start()

    @pl.when(is_kv)
    def _():
        scale = rows_scale(info[START], count)

        def products(cols, partial, at, kv):
            o_part, dq_part = partial[0][:, at], partial[1][:, at]
            ph = (d[:, cols].astype(F32) * scale).astype(BF16)
            return (
                ((o_part + dot(q[:, cols], kv, 1, 0)) * scale).astype(BF16),
                (dq_part + dot(ph, kv, 1, 1)).astype(BF16),
            )

        each_head(products, o_hbm, dq_hbm)

    @pl.when(jnp.logical_not(is_kv))
    def _():
        def products(cols, partial, at, gr):
            dk_part, dv_part = partial[2][:, at], partial[3][:, at]
            return (
                (dk_part + dot(v[:, cols], gr, 1, 1)).astype(BF16),
                (dv_part + dot(k[:, cols], gr, 1, 0)).astype(BF16),
            )

        each_head(products, dk_hbm, dv_hbm)

    for step in range(len(steps)):
        for copy in copies(step, o_hbm, dq_hbm):
            copy.wait()


def apply_states(info, args, partials, early, kinds, arrays, outs, after=()):
    count, width = args[0].shape
    quarter = width // DH // 4
    filled = () if outs is None else tuple(outs)
    partials = [x for kind in kinds for x in partials[kind]]
    first_out = 5 + len(partials) + len(arrays)
    columns = len(kinds) * quarter * DH
    return pl.pallas_call(
        functools.partial(
            apply_kernel, early, kinds, len(arrays) // len(kinds), quarter, len(filled), len(after)
        ),
        out_shape=[jax.ShapeDtypeStruct((count, width), BF16)] * 4
        + [jax.ShapeDtypeStruct((quarter, DH, DH), F32)],
        in_specs=[IN_SMEM]
        + [IN_VMEM] * (4 + len(partials) + len(arrays))
        + [IN_HBM] * len(filled)
        + [IN_VMEM] * len(after),
        out_specs=[IN_HBM] * 4 + [IN_VMEM],
        scratch_shapes=[
            pltpu.VMEM((count, columns), BF16),
            pltpu.VMEM((count, columns), BF16),
            pltpu.SemaphoreType.DMA((columns // (4 * DH), 2)),
        ],
        input_output_aliases={first_out + n: n for n in range(len(filled))},
        compiler_params=pltpu.CompilerParams(vmem_limit_bytes=8 * MIB),
        cost_estimate=SMALL,
        name="apply",
    )(info, *args, *partials, *arrays, *filled, *after)


def prepare_kernel(early, n_after, info, *refs):
    near, f_own, f_got, f_got_give, f_keep, f_other, s_own, s_got, s_keep, s_other = refs[:10]
    across, mine, theirs, rest_mine, rest_theirs = refs[10 + n_after :]
    quarter = near.shape[0]
    is_kv = (info[EARLY_KV] == 1) if early else (info[EARLY_KV] != 1)
    is_first = (info[EVEN] == 1) == is_kv
    takes_near = (info[INNER] == 1) if early else (info[INNER] != 1)
    after_row = is_kv == (info[ROW] == 1)
    after_core = is_kv == (info[CORE] == 1)
    for i in range(quarter):
        val = jnp.where(takes_near, near[i], 0.0)
        keep = jnp.where(is_first, f_keep[i], s_keep[i])
        other = jnp.where(is_first, f_other[i], s_other[i])
        own = jnp.where(is_first, f_own[i], s_own[i])
        got = jnp.where(is_first, f_got[i], s_got[i])
        across[i] = val + jnp.where(after_row, 0.0, keep)
        here = val + jnp.where(after_row, other, 0.0)
        mine[i] = here + jnp.where(after_core, got, 0.0)
        theirs[i] = here + jnp.where(after_core, 0.0, own)
        own = jnp.where(is_first, f_own[quarter + i], s_own[quarter + i])
        got = jnp.where(is_first, f_got_give[i], s_got[quarter + i])
        rest_mine[i] = jnp.where(after_core, got, 0.0)
        rest_theirs[i] = jnp.where(after_core, 0.0, own)


def prepare(info, early, near, f, s, after):
    return pl.pallas_call(
        functools.partial(prepare_kernel, early, len(after)),
        out_shape=[jax.ShapeDtypeStruct(near.shape, F32)] * 5,
        in_specs=[IN_SMEM] + [IN_VMEM] * (10 + len(after)),
        out_specs=[IN_VMEM] * 5,
        compiler_params=pltpu.CompilerParams(vmem_limit_bytes=4 * MIB),
        cost_estimate=SMALL,
        name="prepare",
    )(info, near, *f, *s, *after)


def send(array, pairs):
    return lax.ppermute(array, "seq", pairs)


def plane_scan(planes, kv, qg):
    def scan(x, sign):
        def shift(x, by):
            pairs = [(a, a + sign * by) for a in range(planes) if 0 <= a + sign * by < planes]
            return send(x, spread_pairs(pairs))

        x, by = shift(x, 1), 1
        while by < planes:
            x, by = x + shift(x, by), 2 * by
        return x

    return scan(kv, 1), scan(qg, -1)


def spread_pairs(pairs):
    return [(4 * a + i, 4 * b + i) for a, b in pairs for i in range(4)]


def body(query, key_in, value, d_out):
    args = (query, key_in, value, d_out)
    count, width = query.shape
    heads = width // DH
    size, place = lax.axis_size("seq"), lax.axis_index("seq")
    planes = size // 4
    core, row, plane = place % 2, (place // 2) % 2, place // 4
    even = plane % 2 == 0
    early_kv = plane < planes // 2
    inner = (plane == 1) | (plane == 2) | (planes != 4)
    info = jnp.stack([core, row, even, early_kv, place * count, inner]).astype(jnp.int32)
    core_swap = [(i, i ^ 1) for i in range(size)]
    row_swap = [(i, i ^ 2) for i in range(size)]
    far_args = tuple(pltpu.with_memory_space_constraint(x, pltpu.HBM) for x in args)

    quarter = heads // 4
    cuts = slice(0, quarter // 2), slice(quarter // 2, quarter)

    def halves(own, got):
        return own[:quarter] + got[:quarter], own[quarter:] + got[quarter:]

    kinds = (0, 0), (0, 1), (1, 0), (1, 1)
    sib_keep, sib_give, left, right = first_state(info, far_args)
    got_give = send(sib_give, core_swap)
    got_keep = send(sib_keep, core_swap)
    f_own = own_state(info, left, right)
    f_give = f_own[quarter:] + got_give
    f_keep = f_own[:quarter] + got_keep
    f_other = send(f_give, row_swap)
    s_sib, s_own, *args = second_states(info, far_args, (f_give,))
    part_a, zero = local_part(info, args, kinds[:1], 0.0, (s_own,))
    s_got = send(s_sib, core_swap)
    s_keep, s_give = halves(s_own, s_got)
    f_total = f_keep + f_other + zero
    s_give, f_total = lax.optimization_barrier((s_give, f_total))
    s_other = send(s_give, row_swap)
    f = f_own, got_keep, got_give, f_keep, f_other
    s = s_own, s_got, s_keep, s_other
    part_b, inside = local_part(info, args, kinds[1:], 1.0, (s_give,))
    partials = part_a | part_b
    if planes == 4:
        near = send(f_total, spread_pairs([(0, 1), (1, 0), (2, 3), (3, 2)]))
        pair = jnp.where(inside > 0.0, s_keep + s_other + near, 0.0)
        middle = send(pair, spread_pairs([(1, 2), (2, 1)]) + core_swap[:4] + core_swap[-4:])
        outer = send(middle, spread_pairs([(0, 1), (1, 0), (2, 3), (3, 2)]))
        coming = middle + outer
    else:
        s_total = s_keep + s_other
        kv, qg = plane_scan(
            planes, jnp.where(even, f_total, s_total), jnp.where(even, s_total, f_total)
        )
        near = pair = jnp.where(early_kv, kv, qg)
        coming = jnp.where(early_kv, qg, kv)
    across, mine, theirs, rest_mine, rest_theirs = prepare(info, True, near, f, s, ())

    finish = functools.partial(apply_states, info, args, partials)
    kept_heads, other_heads = kinds[0::2], kinds[1::2]
    t_other = send(across, row_swap)
    t_kept = mine, send(theirs, core_swap)
    late = prepare(info, False, near, f, s, (across,))
    *outs, zero = finish(True, kept_heads, t_kept, None, (across, late[0]))
    t_rest = t_other + rest_mine + zero, send(t_other + rest_theirs, core_swap)

    across = coming + late[0]
    u_other = send(across, row_swap)
    u_kept = [coming[cut] + late[1][cut] for cut in cuts]
    u_kept += [send(coming[cut] + late[2][cut], core_swap) for cut in cuts]
    *outs, _ = finish(True, other_heads, t_rest, outs, (across,))
    *outs, zero = finish(False, kept_heads, u_kept, outs)
    u_rest = u_other + late[3] + zero, send(u_other + late[4], core_swap)
    *outs, _ = finish(False, other_heads, u_rest, outs)
    return tuple(outs)


def solution(mesh):
    spec = P(("group", "seq"), None)
    return jax.shard_map(
        body, mesh=mesh, in_specs=(spec,) * 4, out_specs=(spec,) * 4, check_vma=False
    )
```

```python
import functools

import jax
import jax.numpy as jnp
from jax import lax
from jax.experimental import pallas as pl
from jax.experimental.pallas import tpu as pltpu
from jax.sharding import PartitionSpec as P

DH = 128
F32 = jnp.float32
BF16 = jnp.bfloat16
MIB = 2**20
SMALL = pl.CostEstimate(flops=1, bytes_accessed=1, transcendentals=0)

CORE, ROW, EVEN, EARLY_KV, START, INNER = range(6)

IN_SMEM = pl.BlockSpec(memory_space=pltpu.SMEM)
IN_VMEM = pl.BlockSpec(memory_space=pltpu.VMEM)
IN_HBM = pl.BlockSpec(memory_space=pltpu.HBM)


def rows_scale(start, count):
    where = start + lax.broadcasted_iota(jnp.int32, (count, DH), 0)
    return 1.0 / jnp.sqrt(DH * (where.astype(F32) + 1.0))


def dot(a, b, ca, cb):
    return lax.dot_general(a, b, (((ca,), (cb,)), ((), ())), preferred_element_type=F32)


def first_head(info, side, part, quarter):
    core = info[CORE] if side == 0 else 1 - info[CORE]
    row = info[ROW] if part == 0 else 1 - info[ROW]
    return (core * 2 + row) * quarter


def half_cols(info, side, width):
    core = info[CORE] if side == 0 else 1 - info[CORE]
    half = width // 2
    return pl.multiple_of(core * half, half)


def state_products(is_kv, side, quarter, info, q, k, v, d, out):
    count = q.shape[0]
    pieces = out if isinstance(out, tuple) else (out,)
    each = pieces[0].shape[0]

    def at(n):
        return pieces[n // each].at[n % each]

    @pl.when(is_kv)
    def _():
        for part in range(2):
            head = first_head(info, side, part, quarter)
            for i in range(quarter):
                cols = pl.ds(pl.multiple_of((head + i) * DH, DH), DH)
                at(part * quarter + i)[...] = dot(k[:, cols], v[:, cols], 0, 0)

    @pl.when(jnp.logical_not(is_kv))
    def _():
        scale = rows_scale(info[START], count)
        for part in range(2):
            head = first_head(info, side, part, quarter)
            for i in range(quarter):
                cols = pl.ds(pl.multiple_of((head + i) * DH, DH), DH)
                scaled = (d[:, cols].astype(F32) * scale).astype(BF16)
                at(part * quarter + i)[...] = dot(q[:, cols], scaled, 0, 0)


def pair_copies(info, side, width, rows, sems, *pair):
    half = width // 2
    for n, (there, here) in enumerate(pair):
        for step in range(there.shape[0] // rows):
            at = pl.ds(step * rows, rows), pl.ds(half_cols(info, side, width), half)
            yield pltpu.make_async_copy(there.at[at], here.at[at], sems.at[n, step])


def first_kernel(quarter, rows, info, q, k, v, d, keep, give, left, right, sems):
    width = q.shape[1]
    is_kv = info[EVEN] == 1

    def copies(side, a, b):
        return pair_copies(info, side, width, rows, sems.at[side], (a, left), (b, right))

    @pl.when(is_kv)
    def _():
        for side in (1, 0):
            for copy in copies(side, k, v):
                copy.start()

    @pl.when(jnp.logical_not(is_kv))
    def _():
        for side in (1, 0):
            for copy in copies(side, q, d):
                copy.start()

    for copy in copies(1, k, v):
        copy.wait()
    state_products(is_kv, 1, quarter, info, left, left, right, right, (keep, give))
    for copy in copies(0, k, v):
        copy.wait()


def first_state(info, args):
    count, width = args[0].shape
    heads = width // DH
    rows = count // 4
    return pl.pallas_call(
        functools.partial(first_kernel, heads // 4, rows),
        out_shape=[jax.ShapeDtypeStruct((heads // 4, DH, DH), F32)] * 2
        + [jax.ShapeDtypeStruct((count, width), BF16)] * 2,
        in_specs=[IN_SMEM] + [IN_HBM] * 4,
        out_specs=[IN_VMEM] * 4,
        scratch_shapes=[pltpu.SemaphoreType.DMA((2, 2, count // rows))],
        compiler_params=pltpu.CompilerParams(vmem_limit_bytes=4 * MIB),
        cost_estimate=SMALL,
        name="first",
    )(info, *args)


def own_kernel(quarter, info, left, right, out):
    state_products(info[EVEN] == 1, 0, quarter, info, left, left, right, right, out)


def own_state(info, left, right):
    width = left.shape[1]
    heads = width // DH
    return pl.pallas_call(
        functools.partial(own_kernel, heads // 4),
        out_shape=jax.ShapeDtypeStruct((heads // 2, DH, DH), F32),
        in_specs=[IN_SMEM] + [IN_VMEM] * 2,
        out_specs=IN_VMEM,
        compiler_params=pltpu.CompilerParams(vmem_limit_bytes=4 * MIB),
        cost_estimate=SMALL,
        name="own",
    )(info, left, right)


def second_kernel(quarter, rows, n_after, info, q, k, v, d, *refs):
    sib, own, qv, kv, vv, dv, sems = refs[n_after:]
    width = q.shape[1]
    is_kv = info[EVEN] != 1

    def copies(n, side, *pair):
        return pair_copies(info, side, width, rows, sems.at[n], *pair)

    keys, queries = ((k, kv), (v, vv)), ((q, qv), (d, dv))

    def start(*pairs):
        for n, pair in enumerate(pairs):
            for copy in copies(n, 1 - n % 2, *pair):
                copy.start()

    @pl.when(is_kv)
    def _():
        start(keys, keys, queries, queries)

    @pl.when(jnp.logical_not(is_kv))
    def _():
        start(queries, queries, keys, keys)

    for n, out in ((0, sib), (1, own)):
        for copy in copies(n, 1 - n, *keys):
            copy.wait()
        state_products(is_kv, 1 - n, quarter, info, qv, kv, vv, dv, out)
    for n in (2, 3):
        for copy in copies(n, 1 - n % 2, *keys):
            copy.wait()


def second_states(info, args, after):
    count, width = args[0].shape
    heads = width // DH
    rows = count // 4
    return pl.pallas_call(
        functools.partial(second_kernel, heads // 4, rows, len(after)),
        out_shape=[jax.ShapeDtypeStruct((heads // 2, DH, DH), F32)] * 2
        + [jax.ShapeDtypeStruct((count, width), BF16)] * 4,
        in_specs=[IN_SMEM] + [IN_HBM] * 4 + [IN_VMEM] * len(after),
        out_specs=[IN_VMEM] * 6,
        scratch_shapes=[pltpu.SemaphoreType.DMA((4, 2, count // rows))],
        compiler_params=pltpu.CompilerParams(vmem_limit_bytes=4 * MIB),
        cost_estimate=SMALL,
        name="second",
    )(info, *args, *after)


def local_kernel(kinds, quarter, mark, n_after, info, q, k, v, d, *refs):
    *parts, flag = refs[n_after:]
    flag[...] = jnp.full(flag.shape, jnp.where(info[INNER] == 1, mark, 0.0), F32)
    count = q.shape[0]
    two = 2
    scale = rows_scale(info[START], count)
    lower = lax.broadcasted_iota(jnp.int32, (count, count), 1) <= lax.broadcasted_iota(
        jnp.int32, (count, count), 0
    )

    for n, (side, part) in enumerate(kinds):
        first = first_head(info, side, part, quarter)
        o_ref, dq_ref, dk_ref, dv_ref = parts[4 * n : 4 * n + 4]

        def step(g, carry):
            for i in range(two):
                to = pl.ds(pl.multiple_of((g * two + i) * DH, DH), DH)
                cols = pl.ds(pl.multiple_of((first + g * two + i) * DH, DH), DH)
                qh, kh, vh = q[:, cols], k[:, cols], v[:, cols]
                ph = (d[:, cols].astype(F32) * scale).astype(BF16)
                scores = jnp.where(lower, dot(qh, kh, 1, 1), 0.0).astype(BF16)
                back = jnp.where(lower, dot(ph, vh, 1, 1), 0.0).astype(BF16)
                o_ref[:, to] = dot(scores, vh, 1, 0)
                dq_ref[:, to] = dot(back, kh, 1, 0)
                dk_ref[:, to] = dot(back, qh, 0, 0)
                dv_ref[:, to] = dot(scores, ph, 0, 0)
            return carry

        lax.fori_loop(0, quarter // two, step, 0)


def local_part(info, args, kinds, mark, after=()):
    count, width = args[0].shape
    quarter = width // DH // 4
    *parts, flag = pl.pallas_call(
        functools.partial(local_kernel, kinds, quarter, mark, len(after)),
        out_shape=[jax.ShapeDtypeStruct((count, width // 4), F32)] * (4 * len(kinds))
        + [jax.ShapeDtypeStruct((quarter, DH, DH), F32)],
        in_specs=[IN_SMEM] + [IN_VMEM] * (4 + len(after)),
        out_specs=[IN_VMEM] * (4 * len(kinds) + 1),
        compiler_params=pltpu.CompilerParams(vmem_limit_bytes=8 * MIB),
        cost_estimate=SMALL,
        name="local",
    )(info, *args, *after)
    return {kind: parts[4 * n : 4 * n + 4] for n, kind in enumerate(kinds)}, flag


def apply_kernel(early, kinds, pieces, quarter, n_filled, n_after, info, *refs):
    q, k, v, d = refs[:4]
    refs = refs[4:]
    partials = [refs[4 * n : 4 * n + 4] for n in range(len(kinds))]
    refs = refs[4 * len(kinds) :]
    n_states = len(kinds) * pieces
    state_refs, refs = refs[:n_states], refs[n_states + n_filled + n_after :]
    each = quarter // pieces
    o_hbm, dq_hbm, dk_hbm, dv_hbm, *zero, one, other, sems = refs
    for ref in zero:
        ref[...] = jnp.zeros_like(ref)
    count = q.shape[0]
    two = 2
    is_kv = (info[EARLY_KV] == 1) if early else (info[EARLY_KV] != 1)
    steps = [(n, j) for n in range(len(kinds)) for j in range(quarter // two)]
    starts = [first_head(info, side, part, quarter) * DH for side, part in kinds]

    def columns(n, head):
        return pl.multiple_of(starts[n] + head * DH, DH)

    def copies(step, a, b):
        n, j = steps[step]
        here = pl.ds(step * two * DH, two * DH)
        there = pl.ds(pl.multiple_of(starts[n] + j * two * DH, two * DH), two * DH)
        return (
            pltpu.make_async_copy(one.at[:, here], a.at[:, there], sems.at[step, 0]),
            pltpu.make_async_copy(other.at[:, here], b.at[:, there], sems.at[step, 1]),
        )

    def each_head(products, a, b):
        for step, (n, j) in enumerate(steps):
            for i in range(two):
                head = j * two + i
                cols = pl.ds(columns(n, head), DH)
                at = head * DH
                here = slice((step * two + i) * DH, (step * two + i + 1) * DH)
                one[:, here], other[:, here] = products(
                    cols, partials[n], slice(at, at + DH), state_refs[n * pieces + head // each][head % each].astype(BF16)
                )
            for copy in copies(step, a, b):
                copy.start()

    @pl.when(is_kv)
    def _():
        scale = rows_scale(info[START], count)

        def products(cols, partial, at, kv):
            o_part, dq_part = partial[0][:, at], partial[1][:, at]
            ph = (d[:, cols].astype(F32) * scale).astype(BF16)
            return (
                ((o_part + dot(q[:, cols], kv, 1, 0)) * scale).astype(BF16),
                (dq_part + dot(ph, kv, 1, 1)).astype(BF16),
            )

        each_head(products, o_hbm, dq_hbm)

    @pl.when(jnp.logical_not(is_kv))
    def _():
        def products(cols, partial, at, gr):
            dk_part, dv_part = partial[2][:, at], partial[3][:, at]
            return (
                (dk_part + dot(v[:, cols], gr, 1, 1)).astype(BF16),
                (dv_part + dot(k[:, cols], gr, 1, 0)).astype(BF16),
            )

        each_head(products, dk_hbm, dv_hbm)

    for step in range(len(steps)):
        for copy in copies(step, o_hbm, dq_hbm):
            copy.wait()


def apply_states(info, args, partials, early, kinds, arrays, outs, after=(), tells=False):
    count, width = args[0].shape
    quarter = width // DH // 4
    filled = () if outs is None else tuple(outs)
    partials = [x for kind in kinds for x in partials[kind]]
    first_out = 5 + len(partials) + len(arrays)
    columns = len(kinds) * quarter * DH
    return pl.pallas_call(
        functools.partial(
            apply_kernel, early, kinds, len(arrays) // len(kinds), quarter, len(filled), len(after)
        ),
        out_shape=[jax.ShapeDtypeStruct((count, width), BF16)] * 4
        + [jax.ShapeDtypeStruct((quarter, DH, DH), F32)] * tells,
        in_specs=[IN_SMEM]
        + [IN_VMEM] * (4 + len(partials) + len(arrays))
        + [IN_HBM] * len(filled)
        + [IN_VMEM] * len(after),
        out_specs=[IN_HBM] * 4 + [IN_VMEM] * tells,
        scratch_shapes=[
            pltpu.VMEM((count, columns), BF16),
            pltpu.VMEM((count, columns), BF16),
            pltpu.SemaphoreType.DMA((columns // (2 * DH), 2)),
        ],
        input_output_aliases={first_out + n: n for n in range(len(filled))},
        compiler_params=pltpu.CompilerParams(vmem_limit_bytes=8 * MIB),
        cost_estimate=SMALL,
        name="apply",
    )(info, *args, *partials, *arrays, *filled, *after)


def prepare_kernel(early, n_after, info, *refs):
    near, f_own, f_got, f_got_give, f_keep, f_other, s_own, s_got, s_keep, s_other = refs[:10]
    across, mine, theirs, rest_mine, rest_theirs = refs[10 + n_after :]
    quarter = near.shape[0]
    is_kv = (info[EARLY_KV] == 1) if early else (info[EARLY_KV] != 1)
    is_first = (info[EVEN] == 1) == is_kv
    takes_near = (info[INNER] == 1) if early else (info[INNER] != 1)
    after_row = is_kv == (info[ROW] == 1)
    after_core = is_kv == (info[CORE] == 1)
    for i in range(quarter):
        val = jnp.where(takes_near, near[i], 0.0)
        keep = jnp.where(is_first, f_keep[i], s_keep[i])
        other = jnp.where(is_first, f_other[i], s_other[i])
        own = jnp.where(is_first, f_own[i], s_own[i])
        got = jnp.where(is_first, f_got[i], s_got[i])
        across[i] = val + jnp.where(after_row, 0.0, keep)
        here = val + jnp.where(after_row, other, 0.0)
        mine[i] = here + jnp.where(after_core, got, 0.0)
        theirs[i] = here + jnp.where(after_core, 0.0, own)
        own = jnp.where(is_first, f_own[quarter + i], s_own[quarter + i])
        got = jnp.where(is_first, f_got_give[i], s_got[quarter + i])
        rest_mine[i] = jnp.where(after_core, got, 0.0)
        rest_theirs[i] = jnp.where(after_core, 0.0, own)


def prepare(info, early, near, f, s, after):
    return pl.pallas_call(
        functools.partial(prepare_kernel, early, len(after)),
        out_shape=[jax.ShapeDtypeStruct(near.shape, F32)] * 5,
        in_specs=[IN_SMEM] + [IN_VMEM] * (10 + len(after)),
        out_specs=[IN_VMEM] * 5,
        compiler_params=pltpu.CompilerParams(vmem_limit_bytes=4 * MIB),
        cost_estimate=SMALL,
        name="prepare",
    )(info, near, *f, *s, *after)


def send(array, pairs):
    return lax.ppermute(array, "seq", pairs)


def plane_scan(planes, kv, qg):
    def scan(x, sign):
        def shift(x, by):
            pairs = [(a, a + sign * by) for a in range(planes) if 0 <= a + sign * by < planes]
            return send(x, spread_pairs(pairs))

        x, by = shift(x, 1), 1
        while by < planes:
            x, by = x + shift(x, by), 2 * by
        return x

    return scan(kv, 1), scan(qg, -1)


def spread_pairs(pairs):
    return [(4 * a + i, 4 * b + i) for a, b in pairs for i in range(4)]


def body(query, key_in, value, d_out):
    args = (query, key_in, value, d_out)
    count, width = query.shape
    heads = width // DH
    size, place = lax.axis_size("seq"), lax.axis_index("seq")
    planes = size // 4
    core, row, plane = place % 2, (place // 2) % 2, place // 4
    even = plane % 2 == 0
    early_kv = plane < planes // 2
    inner = (plane == 1) | (plane == 2) | (planes != 4)
    info = jnp.stack([core, row, even, early_kv, place * count, inner]).astype(jnp.int32)
    core_swap = [(i, i ^ 1) for i in range(size)]
    row_swap = [(i, i ^ 2) for i in range(size)]
    far_args = tuple(pltpu.with_memory_space_constraint(x, pltpu.HBM) for x in args)

    quarter = heads // 4
    cuts = slice(0, quarter // 2), slice(quarter // 2, quarter)

    def halves(own, got):
        return own[:quarter] + got[:quarter], own[quarter:] + got[quarter:]

    kinds = (0, 0), (0, 1), (1, 0), (1, 1)
    sib_keep, sib_give, left, right = first_state(info, far_args)
    got_give = send(sib_give, core_swap)
    got_keep = send(sib_keep, core_swap)
    f_own = own_state(info, left, right)
    f_give = f_own[quarter:] + got_give
    f_keep = f_own[:quarter] + got_keep
    f_other = send(f_give, row_swap)
    s_sib, s_own, *args = second_states(info, far_args, (f_give,))
    part_a, zero = local_part(info, args, kinds[:1], 0.0, (s_own,))
    s_got = send(s_sib, core_swap)
    s_keep, s_give = halves(s_own, s_got)
    f_total = f_keep + f_other + zero
    s_give, f_total = lax.optimization_barrier((s_give, f_total))
    s_other = send(s_give, row_swap)
    f = f_own, got_keep, got_give, f_keep, f_other
    s = s_own, s_got, s_keep, s_other
    part_b, inside = local_part(info, args, kinds[1:], 1.0, (s_give,))
    partials = part_a | part_b
    if planes == 4:
        near = send(f_total, spread_pairs([(0, 1), (1, 0), (2, 3), (3, 2)]))
        pair = jnp.where(inside > 0.0, s_keep + s_other + near, 0.0)
        middle = send(pair, spread_pairs([(1, 2), (2, 1)]) + core_swap[:4] + core_swap[-4:])
        outer = send(middle, spread_pairs([(0, 1), (1, 0), (2, 3), (3, 2)]))
        coming = middle + outer
    else:
        s_total = s_keep + s_other
        kv, qg = plane_scan(
            planes, jnp.where(even, f_total, s_total), jnp.where(even, s_total, f_total)
        )
        near = pair = jnp.where(early_kv, kv, qg)
        coming = jnp.where(early_kv, qg, kv)
    across, mine, theirs, rest_mine, rest_theirs = prepare(info, True, near, f, s, ())

    finish = functools.partial(apply_states, info, args, partials)
    kept_heads, other_heads = kinds[0::2], kinds[1::2]
    t_other = send(across, row_swap)
    t_kept = mine, send(theirs, core_swap)
    late = prepare(info, False, near, f, s, (across,))
    *outs, zero = finish(True, kept_heads, t_kept, None, (across, late[0]), True)
    t_rest = t_other + rest_mine + zero, send(t_other + rest_theirs, core_swap)

    across = coming + late[0]
    u_other = send(across, row_swap)
    u_kept = [coming[cut] + late[1][cut] for cut in cuts]
    u_kept += [send(coming[cut] + late[2][cut], core_swap) for cut in cuts]
    outs = finish(True, other_heads, t_rest, outs, (across,))
    *outs, zero = finish(False, kept_heads, u_kept, outs, (), True)
    u_rest = u_other + late[3] + zero, send(u_other + late[4], core_swap)
    outs = finish(False, other_heads, u_rest, outs)
    return tuple(outs)


def solution(mesh):
    spec = P(("group", "seq"), None)
    return jax.shard_map(
        body, mesh=mesh, in_specs=(spec,) * 4, out_specs=(spec,) * 4, check_vma=False
    )
```

```python
import functools

import jax
import jax.numpy as jnp
from jax import lax
from jax.experimental import pallas as pl
from jax.experimental.pallas import tpu as pltpu
from jax.sharding import PartitionSpec as P

DH = 128
F32 = jnp.float32
BF16 = jnp.bfloat16
MIB = 2**20
SMALL = pl.CostEstimate(flops=1, bytes_accessed=1, transcendentals=0)

CORE, ROW, EVEN, EARLY_KV, START, INNER = range(6)

IN_SMEM = pl.BlockSpec(memory_space=pltpu.SMEM)
IN_VMEM = pl.BlockSpec(memory_space=pltpu.VMEM)
IN_HBM = pl.BlockSpec(memory_space=pltpu.HBM)


def rows_scale(start, count):
    where = start + lax.broadcasted_iota(jnp.int32, (count, DH), 0)
    return 1.0 / jnp.sqrt(DH * (where.astype(F32) + 1.0))


def dot(a, b, ca, cb):
    return lax.dot_general(a, b, (((ca,), (cb,)), ((), ())), preferred_element_type=F32)


def first_head(info, side, part, quarter):
    core = info[CORE] if side == 0 else 1 - info[CORE]
    row = info[ROW] if part == 0 else 1 - info[ROW]
    return (core * 2 + row) * quarter


def half_cols(info, side, width):
    core = info[CORE] if side == 0 else 1 - info[CORE]
    half = width // 2
    return pl.multiple_of(core * half, half)


def state_products(is_kv, side, quarter, info, q, k, v, d, out):
    count = q.shape[0]
    pieces = out if isinstance(out, tuple) else (out,)
    each = pieces[0].shape[0]

    def at(n):
        return pieces[n // each].at[n % each]

    @pl.when(is_kv)
    def _():
        for part in range(2):
            head = first_head(info, side, part, quarter)
            for i in range(quarter):
                cols = pl.ds(pl.multiple_of((head + i) * DH, DH), DH)
                at(part * quarter + i)[...] = dot(k[:, cols], v[:, cols], 0, 0)

    @pl.when(jnp.logical_not(is_kv))
    def _():
        scale = rows_scale(info[START], count)
        for part in range(2):
            head = first_head(info, side, part, quarter)
            for i in range(quarter):
                cols = pl.ds(pl.multiple_of((head + i) * DH, DH), DH)
                scaled = (d[:, cols].astype(F32) * scale).astype(BF16)
                at(part * quarter + i)[...] = dot(q[:, cols], scaled, 0, 0)


def pair_copies(info, side, width, rows, sems, *pair):
    half = width // 2
    for n, (there, here) in enumerate(pair):
        for step in range(there.shape[0] // rows):
            at = pl.ds(step * rows, rows), pl.ds(half_cols(info, side, width), half)
            yield pltpu.make_async_copy(there.at[at], here.at[at], sems.at[n, step])


def first_kernel(quarter, rows, info, q, k, v, d, keep, give, left, right, sems):
    width = q.shape[1]
    is_kv = info[EVEN] == 1

    def copies(side, a, b):
        return pair_copies(info, side, width, rows, sems.at[side], (a, left), (b, right))

    @pl.when(is_kv)
    def _():
        for side in (1, 0):
            for copy in copies(side, k, v):
                copy.start()

    @pl.when(jnp.logical_not(is_kv))
    def _():
        for side in (1, 0):
            for copy in copies(side, q, d):
                copy.start()

    for copy in copies(1, k, v):
        copy.wait()
    state_products(is_kv, 1, quarter, info, left, left, right, right, (keep, give))
    for copy in copies(0, k, v):
        copy.wait()


def first_state(info, args):
    count, width = args[0].shape
    heads = width // DH
    rows = count // 1
    return pl.pallas_call(
        functools.partial(first_kernel, heads // 4, rows),
        out_shape=[jax.ShapeDtypeStruct((heads // 4, DH, DH), F32)] * 2
        + [jax.ShapeDtypeStruct((count, width), BF16)] * 2,
        in_specs=[IN_SMEM] + [IN_HBM] * 4,
        out_specs=[IN_VMEM] * 4,
        scratch_shapes=[pltpu.SemaphoreType.DMA((2, 2, count // rows))],
        compiler_params=pltpu.CompilerParams(vmem_limit_bytes=4 * MIB),
        cost_estimate=SMALL,
        name="first",
    )(info, *args)


def own_kernel(quarter, info, left, right, out):
    state_products(info[EVEN] == 1, 0, quarter, info, left, left, right, right, out)


def own_state(info, left, right):
    width = left.shape[1]
    heads = width // DH
    return pl.pallas_call(
        functools.partial(own_kernel, heads // 4),
        out_shape=jax.ShapeDtypeStruct((heads // 2, DH, DH), F32),
        in_specs=[IN_SMEM] + [IN_VMEM] * 2,
        out_specs=IN_VMEM,
        compiler_params=pltpu.CompilerParams(vmem_limit_bytes=4 * MIB),
        cost_estimate=SMALL,
        name="own",
    )(info, left, right)


def second_kernel(quarter, rows, n_after, info, q, k, v, d, *refs):
    sib, own, qv, kv, vv, dv, sems = refs[n_after:]
    width = q.shape[1]
    is_kv = info[EVEN] != 1

    def copies(n, side, *pair):
        return pair_copies(info, side, width, rows, sems.at[n], *pair)

    keys, queries = ((k, kv), (v, vv)), ((q, qv), (d, dv))

    def start(*pairs):
        for n, pair in enumerate(pairs):
            for copy in copies(n, 1 - n % 2, *pair):
                copy.start()

    @pl.when(is_kv)
    def _():
        start(keys, keys, queries, queries)

    @pl.when(jnp.logical_not(is_kv))
    def _():
        start(queries, queries, keys, keys)

    for n, out in ((0, sib), (1, own)):
        for copy in copies(n, 1 - n, *keys):
            copy.wait()
        state_products(is_kv, 1 - n, quarter, info, qv, kv, vv, dv, out)
    for n in (2, 3):
        for copy in copies(n, 1 - n % 2, *keys):
            copy.wait()


def second_states(info, args, after):
    count, width = args[0].shape
    heads = width // DH
    rows = count // 1
    return pl.pallas_call(
        functools.partial(second_kernel, heads // 4, rows, len(after)),
        out_shape=[jax.ShapeDtypeStruct((heads // 2, DH, DH), F32)] * 2
        + [jax.ShapeDtypeStruct((count, width), BF16)] * 4,
        in_specs=[IN_SMEM] + [IN_HBM] * 4 + [IN_VMEM] * len(after),
        out_specs=[IN_VMEM] * 6,
        scratch_shapes=[pltpu.SemaphoreType.DMA((4, 2, count // rows))],
        compiler_params=pltpu.CompilerParams(vmem_limit_bytes=4 * MIB),
        cost_estimate=SMALL,
        name="second",
    )(info, *args, *after)


def local_kernel(kinds, quarter, mark, n_after, info, q, k, v, d, *refs):
    *parts, flag = refs[n_after:]
    flag[...] = jnp.full(flag.shape, jnp.where(info[INNER] == 1, mark, 0.0), F32)
    count = q.shape[0]
    half = count // 2
    two = 2
    scale = rows_scale(info[START], count)
    lower = lax.broadcasted_iota(jnp.int32, (count, count), 1) <= lax.broadcasted_iota(
        jnp.int32, (count, count), 0
    )

    for n, (side, part) in enumerate(kinds):
        first = first_head(info, side, part, quarter)
        o_ref, dq_ref, dk_ref, dv_ref = parts[4 * n : 4 * n + 4]

        def step(g, carry):
            for i in range(two):
                to = pl.ds(pl.multiple_of((g * two + i) * DH, DH), DH)
                cols = pl.ds(pl.multiple_of((first + g * two + i) * DH, DH), DH)
                qh, kh, vh = q[:, cols], k[:, cols], v[:, cols]
                ph = (d[:, cols].astype(F32) * scale).astype(BF16)
                top, bottom = slice(0, half), slice(half, count)
                s0 = jnp.where(lower[top, top], dot(qh[top], kh[top], 1, 1), 0.0).astype(BF16)
                s1 = jnp.where(lower[bottom], dot(qh[bottom], kh, 1, 1), 0.0).astype(BF16)
                b0 = jnp.where(lower[top, top], dot(ph[top], vh[top], 1, 1), 0.0).astype(BF16)
                b1 = jnp.where(lower[bottom], dot(ph[bottom], vh, 1, 1), 0.0).astype(BF16)
                o_ref[top, to] = dot(s0, vh[top], 1, 0)
                o_ref[bottom, to] = dot(s1, vh, 1, 0)
                dq_ref[top, to] = dot(b0, kh[top], 1, 0)
                dq_ref[bottom, to] = dot(b1, kh, 1, 0)
                dk_ref[top, to] = dot(b0, qh[top], 0, 0) + dot(b1[:, top], qh[bottom], 0, 0)
                dk_ref[bottom, to] = dot(b1[:, bottom], qh[bottom], 0, 0)
                dv_ref[top, to] = dot(s0, ph[top], 0, 0) + dot(s1[:, top], ph[bottom], 0, 0)
                dv_ref[bottom, to] = dot(s1[:, bottom], ph[bottom], 0, 0)
            return carry

        lax.fori_loop(0, quarter // two, step, 0)


def local_part(info, args, kinds, mark, after=()):
    count, width = args[0].shape
    quarter = width // DH // 4
    *parts, flag = pl.pallas_call(
        functools.partial(local_kernel, kinds, quarter, mark, len(after)),
        out_shape=[jax.ShapeDtypeStruct((count, width // 4), F32)] * (4 * len(kinds))
        + [jax.ShapeDtypeStruct((quarter, DH, DH), F32)],
        in_specs=[IN_SMEM] + [IN_VMEM] * (4 + len(after)),
        out_specs=[IN_VMEM] * (4 * len(kinds) + 1),
        compiler_params=pltpu.CompilerParams(vmem_limit_bytes=8 * MIB),
        cost_estimate=SMALL,
        name="local",
    )(info, *args, *after)
    return {kind: parts[4 * n : 4 * n + 4] for n, kind in enumerate(kinds)}, flag


def apply_kernel(early, kinds, pieces, quarter, n_filled, n_after, info, *refs):
    q, k, v, d = refs[:4]
    refs = refs[4:]
    partials = [refs[4 * n : 4 * n + 4] for n in range(len(kinds))]
    refs = refs[4 * len(kinds) :]
    n_states = len(kinds) * pieces
    state_refs, refs = refs[:n_states], refs[n_states + n_filled + n_after :]
    each = quarter // pieces
    o_hbm, dq_hbm, dk_hbm, dv_hbm, *zero, one, other, sems = refs
    for ref in zero:
        ref[...] = jnp.zeros_like(ref)
    count = q.shape[0]
    two = 2
    is_kv = (info[EARLY_KV] == 1) if early else (info[EARLY_KV] != 1)
    steps = [(n, j) for n in range(len(kinds)) for j in range(quarter // two)]
    starts = [first_head(info, side, part, quarter) * DH for side, part in kinds]

    def columns(n, head):
        return pl.multiple_of(starts[n] + head * DH, DH)

    def copies(step, a, b):
        n, j = steps[step]
        here = pl.ds(step * two * DH, two * DH)
        there = pl.ds(pl.multiple_of(starts[n] + j * two * DH, two * DH), two * DH)
        return (
            pltpu.make_async_copy(one.at[:, here], a.at[:, there], sems.at[step, 0]),
            pltpu.make_async_copy(other.at[:, here], b.at[:, there], sems.at[step, 1]),
        )

    def each_head(products, a, b):
        for step, (n, j) in enumerate(steps):
            for i in range(two):
                head = j * two + i
                cols = pl.ds(columns(n, head), DH)
                at = head * DH
                here = slice((step * two + i) * DH, (step * two + i + 1) * DH)
                one[:, here], other[:, here] = products(
                    cols, partials[n], slice(at, at + DH), state_refs[n * pieces + head // each][head % each].astype(BF16)
                )
            for copy in copies(step, a, b):
                copy.start()

    @pl.when(is_kv)
    def _():
        scale = rows_scale(info[START], count)

        def products(cols, partial, at, kv):
            o_part, dq_part = partial[0][:, at], partial[1][:, at]
            ph = (d[:, cols].astype(F32) * scale).astype(BF16)
            return (
                ((o_part + dot(q[:, cols], kv, 1, 0)) * scale).astype(BF16),
                (dq_part + dot(ph, kv, 1, 1)).astype(BF16),
            )

        each_head(products, o_hbm, dq_hbm)

    @pl.when(jnp.logical_not(is_kv))
    def _():
        def products(cols, partial, at, gr):
            dk_part, dv_part = partial[2][:, at], partial[3][:, at]
            return (
                (dk_part + dot(v[:, cols], gr, 1, 1)).astype(BF16),
                (dv_part + dot(k[:, cols], gr, 1, 0)).astype(BF16),
            )

        each_head(products, dk_hbm, dv_hbm)

    for step in range(len(steps)):
        for copy in copies(step, o_hbm, dq_hbm):
            copy.wait()


def apply_states(info, args, partials, early, kinds, arrays, outs, after=(), tells=False):
    count, width = args[0].shape
    quarter = width // DH // 4
    filled = () if outs is None else tuple(outs)
    partials = [x for kind in kinds for x in partials[kind]]
    first_out = 5 + len(partials) + len(arrays)
    columns = len(kinds) * quarter * DH
    return pl.pallas_call(
        functools.partial(
            apply_kernel, early, kinds, len(arrays) // len(kinds), quarter, len(filled), len(after)
        ),
        out_shape=[jax.ShapeDtypeStruct((count, width), BF16)] * 4
        + [jax.ShapeDtypeStruct((quarter, DH, DH), F32)] * tells,
        in_specs=[IN_SMEM]
        + [IN_VMEM] * (4 + len(partials) + len(arrays))
        + [IN_HBM] * len(filled)
        + [IN_VMEM] * len(after),
        out_specs=[IN_HBM] * 4 + [IN_VMEM] * tells,
        scratch_shapes=[
            pltpu.VMEM((count, columns), BF16),
            pltpu.VMEM((count, columns), BF16),
            pltpu.SemaphoreType.DMA((columns // (2 * DH), 2)),
        ],
        input_output_aliases={first_out + n: n for n in range(len(filled))},
        compiler_params=pltpu.CompilerParams(vmem_limit_bytes=8 * MIB),
        cost_estimate=SMALL,
        name="apply",
    )(info, *args, *partials, *arrays, *filled, *after)


def prepare_kernel(early, n_after, info, *refs):
    near, f_own, f_got, f_got_give, f_keep, f_other, s_own, s_got, s_keep, s_other = refs[:10]
    across, mine, theirs, rest_mine, rest_theirs = refs[10 + n_after :]
    quarter = near.shape[0]
    is_kv = (info[EARLY_KV] == 1) if early else (info[EARLY_KV] != 1)
    is_first = (info[EVEN] == 1) == is_kv
    takes_near = (info[INNER] == 1) if early else (info[INNER] != 1)
    after_row = is_kv == (info[ROW] == 1)
    after_core = is_kv == (info[CORE] == 1)
    for i in range(quarter):
        val = jnp.where(takes_near, near[i], 0.0)
        keep = jnp.where(is_first, f_keep[i], s_keep[i])
        other = jnp.where(is_first, f_other[i], s_other[i])
        own = jnp.where(is_first, f_own[i], s_own[i])
        got = jnp.where(is_first, f_got[i], s_got[i])
        across[i] = val + jnp.where(after_row, 0.0, keep)
        here = val + jnp.where(after_row, other, 0.0)
        mine[i] = here + jnp.where(after_core, got, 0.0)
        theirs[i] = here + jnp.where(after_core, 0.0, own)
        own = jnp.where(is_first, f_own[quarter + i], s_own[quarter + i])
        got = jnp.where(is_first, f_got_give[i], s_got[quarter + i])
        rest_mine[i] = jnp.where(after_core, got, 0.0)
        rest_theirs[i] = jnp.where(after_core, 0.0, own)


def prepare(info, early, near, f, s, after):
    return pl.pallas_call(
        functools.partial(prepare_kernel, early, len(after)),
        out_shape=[jax.ShapeDtypeStruct(near.shape, F32)] * 5,
        in_specs=[IN_SMEM] + [IN_VMEM] * (10 + len(after)),
        out_specs=[IN_VMEM] * 5,
        compiler_params=pltpu.CompilerParams(vmem_limit_bytes=4 * MIB),
        cost_estimate=SMALL,
        name="prepare",
    )(info, near, *f, *s, *after)


def send(array, pairs):
    return lax.ppermute(array, "seq", pairs)


def plane_scan(planes, kv, qg):
    def scan(x, sign):
        def shift(x, by):
            pairs = [(a, a + sign * by) for a in range(planes) if 0 <= a + sign * by < planes]
            return send(x, spread_pairs(pairs))

        x, by = shift(x, 1), 1
        while by < planes:
            x, by = x + shift(x, by), 2 * by
        return x

    return scan(kv, 1), scan(qg, -1)


def spread_pairs(pairs):
    return [(4 * a + i, 4 * b + i) for a, b in pairs for i in range(4)]


def body(query, key_in, value, d_out):
    args = (query, key_in, value, d_out)
    count, width = query.shape
    heads = width // DH
    size, place = lax.axis_size("seq"), lax.axis_index("seq")
    planes = size // 4
    core, row, plane = place % 2, (place // 2) % 2, place // 4
    even = plane % 2 == 0
    early_kv = plane < planes // 2
    inner = (plane == 1) | (plane == 2) | (planes != 4)
    info = jnp.stack([core, row, even, early_kv, place * count, inner]).astype(jnp.int32)
    core_swap = [(i, i ^ 1) for i in range(size)]
    row_swap = [(i, i ^ 2) for i in range(size)]
    far_args = tuple(pltpu.with_memory_space_constraint(x, pltpu.HBM) for x in args)

    quarter = heads // 4
    cuts = slice(0, quarter // 2), slice(quarter // 2, quarter)

    def halves(own, got):
        return own[:quarter] + got[:quarter], own[quarter:] + got[quarter:]

    kinds = (0, 0), (0, 1), (1, 0), (1, 1)
    sib_keep, sib_give, left, right = first_state(info, far_args)
    got_give = send(sib_give, core_swap)
    got_keep = send(sib_keep, core_swap)
    f_own = own_state(info, left, right)
    f_give = f_own[quarter:] + got_give
    f_keep = f_own[:quarter] + got_keep
    f_other = send(f_give, row_swap)
    s_sib, s_own, *args = second_states(info, far_args, (f_give,))
    part_a, zero = local_part(info, args, kinds[:1], 0.0, (s_own,))
    s_got = send(s_sib, core_swap)
    s_keep, s_give = halves(s_own, s_got)
    f_total = f_keep + f_other + zero
    s_give, f_total = lax.optimization_barrier((s_give, f_total))
    s_other = send(s_give, row_swap)
    f = f_own, got_keep, got_give, f_keep, f_other
    s = s_own, s_got, s_keep, s_other
    part_b, inside = local_part(info, args, kinds[1:], 1.0, (s_give,))
    partials = part_a | part_b
    if planes == 4:
        near = send(f_total, spread_pairs([(0, 1), (1, 0), (2, 3), (3, 2)]))
        pair = jnp.where(inside > 0.0, s_keep + s_other + near, 0.0)
        middle = send(pair, spread_pairs([(1, 2), (2, 1)]) + core_swap[:4] + core_swap[-4:])
        outer = send(middle, spread_pairs([(0, 1), (1, 0), (2, 3), (3, 2)]))
        coming = middle + outer
    else:
        s_total = s_keep + s_other
        kv, qg = plane_scan(
            planes, jnp.where(even, f_total, s_total), jnp.where(even, s_total, f_total)
        )
        near = pair = jnp.where(early_kv, kv, qg)
        coming = jnp.where(early_kv, qg, kv)
    across, mine, theirs, rest_mine, rest_theirs = prepare(info, True, near, f, s, ())

    finish = functools.partial(apply_states, info, args, partials)
    kept_heads, other_heads = kinds[0::2], kinds[1::2]
    t_other = send(across, row_swap)
    t_kept = mine, send(theirs, core_swap)
    late = prepare(info, False, near, f, s, (across,))
    *outs, zero = finish(True, kept_heads, t_kept, None, (across, late[0]), True)
    t_rest = t_other + rest_mine + zero, send(t_other + rest_theirs, core_swap)

    across = coming + late[0]
    u_other = send(across, row_swap)
    u_kept = [coming[cut] + late[1][cut] for cut in cuts]
    u_kept += [send(coming[cut] + late[2][cut], core_swap) for cut in cuts]
    outs = finish(True, other_heads, t_rest, outs, (across,))
    *outs, zero = finish(False, kept_heads, u_kept, outs, (), True)
    u_rest = u_other + late[3] + zero, send(u_other + late[4], core_swap)
    outs = finish(False, other_heads, u_rest, outs)
    return tuple(outs)


def solution(mesh):
    spec = P(("group", "seq"), None)
    return jax.shard_map(
        body, mesh=mesh, in_specs=(spec,) * 4, out_specs=(spec,) * 4, check_vma=False
    )
```

```python
import functools

import jax
import jax.numpy as jnp
from jax import lax
from jax.experimental import pallas as pl
from jax.experimental.pallas import tpu as pltpu
from jax.sharding import PartitionSpec as P

DH = 128
F32 = jnp.float32
BF16 = jnp.bfloat16
MIB = 2**20
SMALL = pl.CostEstimate(flops=1, bytes_accessed=1, transcendentals=0)

CORE, ROW, EVEN, EARLY_KV, START, INNER = range(6)

IN_SMEM = pl.BlockSpec(memory_space=pltpu.SMEM)
IN_VMEM = pl.BlockSpec(memory_space=pltpu.VMEM)
IN_HBM = pl.BlockSpec(memory_space=pltpu.HBM)


def rows_scale(start, count):
    where = start + lax.broadcasted_iota(jnp.int32, (count, DH), 0)
    return 1.0 / jnp.sqrt(DH * (where.astype(F32) + 1.0))


def dot(a, b, ca, cb):
    return lax.dot_general(a, b, (((ca,), (cb,)), ((), ())), preferred_element_type=F32)


def first_head(info, side, part, quarter):
    core = info[CORE] if side == 0 else 1 - info[CORE]
    row = info[ROW] if part == 0 else 1 - info[ROW]
    return (core * 2 + row) * quarter


def half_cols(info, side, width):
    core = info[CORE] if side == 0 else 1 - info[CORE]
    half = width // 2
    return pl.multiple_of(core * half, half)


def state_products(is_kv, side, quarter, info, q, k, v, d, out, parts=(0, 1)):
    count = q.shape[0]
    pieces = out if isinstance(out, tuple) else (out,)
    each = pieces[0].shape[0]

    def at(n):
        return pieces[n // each].at[n % each]

    @pl.when(is_kv)
    def _():
        for part in parts:
            head = first_head(info, side, part, quarter)
            for i in range(quarter):
                cols = pl.ds(pl.multiple_of((head + i) * DH, DH), DH)
                at(part * quarter + i)[...] = dot(k[:, cols], v[:, cols], 0, 0)

    @pl.when(jnp.logical_not(is_kv))
    def _():
        scale = rows_scale(info[START], count)
        for part in parts:
            head = first_head(info, side, part, quarter)
            for i in range(quarter):
                cols = pl.ds(pl.multiple_of((head + i) * DH, DH), DH)
                scaled = (d[:, cols].astype(F32) * scale).astype(BF16)
                at(part * quarter + i)[...] = dot(q[:, cols], scaled, 0, 0)


def pair_copies(start, columns, rows, sems, *pair):
    for n, (there, here) in enumerate(pair):
        for step in range(there.shape[0] // rows):
            at = pl.ds(step * rows, rows), pl.ds(start, columns)
            yield pltpu.make_async_copy(there.at[at], here.at[at], sems.at[n, step])


def first_kernel(quarter, rows, info, q, k, v, d, keep, give, left, right, sems):
    width = q.shape[1]
    is_kv = info[EVEN] == 1

    def copies(side, a, b):
        start, columns = half_cols(info, side, width), width // 2
        if side == 0:
            columns = quarter * DH
            start = pl.multiple_of(first_head(info, side, 1, quarter) * DH, columns)
        return pair_copies(start, columns, rows, sems.at[side], (a, left), (b, right))

    @pl.when(is_kv)
    def _():
        for side in (1, 0):
            for copy in copies(side, k, v):
                copy.start()

    @pl.when(jnp.logical_not(is_kv))
    def _():
        for side in (1, 0):
            for copy in copies(side, q, d):
                copy.start()

    for copy in copies(1, k, v):
        copy.wait()
    state_products(is_kv, 1, quarter, info, left, left, right, right, (keep, give))
    for copy in copies(0, k, v):
        copy.wait()


def first_state(info, args):
    count, width = args[0].shape
    heads = width // DH
    rows = count // 1
    return pl.pallas_call(
        functools.partial(first_kernel, heads // 4, rows),
        out_shape=[jax.ShapeDtypeStruct((heads // 4, DH, DH), F32)] * 2
        + [jax.ShapeDtypeStruct((count, width), BF16)] * 2,
        in_specs=[IN_SMEM] + [IN_HBM] * 4,
        out_specs=[IN_VMEM] * 4,
        scratch_shapes=[pltpu.SemaphoreType.DMA((2, 2, count // rows))],
        compiler_params=pltpu.CompilerParams(vmem_limit_bytes=4 * MIB),
        cost_estimate=SMALL,
        name="first",
    )(info, *args)


def own_kernel(quarter, info, left, right, out):
    state_products(info[EVEN] == 1, 0, quarter, info, left, left, right, right, (out, out), (1,))


def own_state(info, left, right):
    width = left.shape[1]
    heads = width // DH
    return pl.pallas_call(
        functools.partial(own_kernel, heads // 4),
        out_shape=jax.ShapeDtypeStruct((heads // 4, DH, DH), F32),
        in_specs=[IN_SMEM] + [IN_VMEM] * 2,
        out_specs=IN_VMEM,
        compiler_params=pltpu.CompilerParams(vmem_limit_bytes=4 * MIB),
        cost_estimate=SMALL,
        name="own",
    )(info, left, right)


def second_kernel(quarter, rows, n_after, info, q, k, v, d, *refs):
    sib, own, kept, qv, kv, vv, dv, sems = refs[n_after:]
    width = q.shape[1]
    is_kv = info[EVEN] != 1

    def copies(n, side, *pair):
        return pair_copies(half_cols(info, side, width), width // 2, rows, sems.at[n], *pair)

    keys, queries = ((k, kv), (v, vv)), ((q, qv), (d, dv))

    def start(*pairs):
        for n, pair in enumerate(pairs):
            for copy in copies(n, 1 - n % 2, *pair):
                copy.start()

    @pl.when(is_kv)
    def _():
        start(keys, keys, queries, queries)

    @pl.when(jnp.logical_not(is_kv))
    def _():
        start(queries, queries, keys, keys)

    for n, out in ((0, sib), (1, own)):
        for copy in copies(n, 1 - n, *keys):
            copy.wait()
        state_products(is_kv, 1 - n, quarter, info, qv, kv, vv, dv, out)
    for n in (2, 3):
        for copy in copies(n, 1 - n % 2, *keys):
            copy.wait()
    is_first = jnp.logical_not(is_kv)
    state_products(is_first, 0, quarter, info, qv, kv, vv, dv, (kept, kept), (0,))


def second_states(info, args, after):
    count, width = args[0].shape
    heads = width // DH
    rows = count // 1
    return pl.pallas_call(
        functools.partial(second_kernel, heads // 4, rows, len(after)),
        out_shape=[jax.ShapeDtypeStruct((heads // 2, DH, DH), F32)] * 2
        + [jax.ShapeDtypeStruct((heads // 4, DH, DH), F32)]
        + [jax.ShapeDtypeStruct((count, width), BF16)] * 4,
        in_specs=[IN_SMEM] + [IN_HBM] * 4 + [IN_VMEM] * len(after),
        out_specs=[IN_VMEM] * 7,
        scratch_shapes=[pltpu.SemaphoreType.DMA((4, 2, count // rows))],
        compiler_params=pltpu.CompilerParams(vmem_limit_bytes=4 * MIB),
        cost_estimate=SMALL,
        name="second",
    )(info, *args, *after)


def local_kernel(kinds, quarter, mark, n_after, info, q, k, v, d, *refs):
    *parts, flag = refs[n_after:]
    flag[...] = jnp.full(flag.shape, jnp.where(info[INNER] == 1, mark, 0.0), F32)
    count = q.shape[0]
    half = count // 2
    two = 2
    scale = rows_scale(info[START], count)
    lower = lax.broadcasted_iota(jnp.int32, (count, count), 1) <= lax.broadcasted_iota(
        jnp.int32, (count, count), 0
    )

    for n, (side, part) in enumerate(kinds):
        first = first_head(info, side, part, quarter)
        o_ref, dq_ref, dk_ref, dv_ref = parts[4 * n : 4 * n + 4]

        def step(g, carry):
            for i in range(two):
                to = pl.ds(pl.multiple_of((g * two + i) * DH, DH), DH)
                cols = pl.ds(pl.multiple_of((first + g * two + i) * DH, DH), DH)
                qh, kh, vh = q[:, cols], k[:, cols], v[:, cols]
                ph = (d[:, cols].astype(F32) * scale).astype(BF16)
                top, bottom = slice(0, half), slice(half, count)
                s0 = jnp.where(lower[top, top], dot(qh[top], kh[top], 1, 1), 0.0).astype(BF16)
                s1 = jnp.where(lower[bottom], dot(qh[bottom], kh, 1, 1), 0.0).astype(BF16)
                b0 = jnp.where(lower[top, top], dot(ph[top], vh[top], 1, 1), 0.0).astype(BF16)
                b1 = jnp.where(lower[bottom], dot(ph[bottom], vh, 1, 1), 0.0).astype(BF16)
                o_ref[top, to] = dot(s0, vh[top], 1, 0)
                o_ref[bottom, to] = dot(s1, vh, 1, 0)
                dq_ref[top, to] = dot(b0, kh[top], 1, 0)
                dq_ref[bottom, to] = dot(b1, kh, 1, 0)
                dk_ref[top, to] = dot(b0, qh[top], 0, 0) + dot(b1[:, top], qh[bottom], 0, 0)
                dk_ref[bottom, to] = dot(b1[:, bottom], qh[bottom], 0, 0)
                dv_ref[top, to] = dot(s0, ph[top], 0, 0) + dot(s1[:, top], ph[bottom], 0, 0)
                dv_ref[bottom, to] = dot(s1[:, bottom], ph[bottom], 0, 0)
            return carry

        lax.fori_loop(0, quarter // two, step, 0)


def local_part(info, args, kinds, mark, after=()):
    count, width = args[0].shape
    quarter = width // DH // 4
    *parts, flag = pl.pallas_call(
        functools.partial(local_kernel, kinds, quarter, mark, len(after)),
        out_shape=[jax.ShapeDtypeStruct((count, width // 4), F32)] * (4 * len(kinds))
        + [jax.ShapeDtypeStruct((quarter, DH, DH), F32)],
        in_specs=[IN_SMEM] + [IN_VMEM] * (4 + len(after)),
        out_specs=[IN_VMEM] * (4 * len(kinds) + 1),
        compiler_params=pltpu.CompilerParams(vmem_limit_bytes=8 * MIB),
        cost_estimate=SMALL,
        name="local",
    )(info, *args, *after)
    return {kind: parts[4 * n : 4 * n + 4] for n, kind in enumerate(kinds)}, flag


def apply_kernel(early, kinds, pieces, quarter, n_filled, n_after, info, *refs):
    q, k, v, d = refs[:4]
    refs = refs[4:]
    partials = [refs[4 * n : 4 * n + 4] for n in range(len(kinds))]
    refs = refs[4 * len(kinds) :]
    n_states = len(kinds) * pieces
    state_refs, refs = refs[:n_states], refs[n_states + n_filled + n_after :]
    each = quarter // pieces
    o_hbm, dq_hbm, dk_hbm, dv_hbm, *zero, one, other, sems = refs
    for ref in zero:
        ref[...] = jnp.zeros_like(ref)
    count = q.shape[0]
    two = 2
    is_kv = (info[EARLY_KV] == 1) if early else (info[EARLY_KV] != 1)
    steps = [(n, j) for n in range(len(kinds)) for j in range(quarter // two)]
    starts = [first_head(info, side, part, quarter) * DH for side, part in kinds]

    def columns(n, head):
        return pl.multiple_of(starts[n] + head * DH, DH)

    def copies(step, a, b):
        n, j = steps[step]
        here = pl.ds(step * two * DH, two * DH)
        there = pl.ds(pl.multiple_of(starts[n] + j * two * DH, two * DH), two * DH)
        return (
            pltpu.make_async_copy(one.at[:, here], a.at[:, there], sems.at[step, 0]),
            pltpu.make_async_copy(other.at[:, here], b.at[:, there], sems.at[step, 1]),
        )

    def each_head(products, a, b):
        for step, (n, j) in enumerate(steps):
            for i in range(two):
                head = j * two + i
                cols = pl.ds(columns(n, head), DH)
                at = head * DH
                here = slice((step * two + i) * DH, (step * two + i + 1) * DH)
                one[:, here], other[:, here] = products(
                    cols, partials[n], slice(at, at + DH), state_refs[n * pieces + head // each][head % each].astype(BF16)
                )
            for copy in copies(step, a, b):
                copy.start()

    @pl.when(is_kv)
    def _():
        scale = rows_scale(info[START], count)

        def products(cols, partial, at, kv):
            o_part, dq_part = partial[0][:, at], partial[1][:, at]
            ph = (d[:, cols].astype(F32) * scale).astype(BF16)
            return (
                ((o_part + dot(q[:, cols], kv, 1, 0)) * scale).astype(BF16),
                (dq_part + dot(ph, kv, 1, 1)).astype(BF16),
            )

        each_head(products, o_hbm, dq_hbm)

    @pl.when(jnp.logical_not(is_kv))
    def _():
        def products(cols, partial, at, gr):
            dk_part, dv_part = partial[2][:, at], partial[3][:, at]
            return (
                (dk_part + dot(v[:, cols], gr, 1, 1)).astype(BF16),
                (dv_part + dot(k[:, cols], gr, 1, 0)).astype(BF16),
            )

        each_head(products, dk_hbm, dv_hbm)

    for step in range(len(steps)):
        for copy in copies(step, o_hbm, dq_hbm):
            copy.wait()


def apply_states(info, args, partials, early, kinds, arrays, outs, after=(), tells=False):
    count, width = args[0].shape
    quarter = width // DH // 4
    filled = () if outs is None else tuple(outs)
    partials = [x for kind in kinds for x in partials[kind]]
    first_out = 5 + len(partials) + len(arrays)
    columns = len(kinds) * quarter * DH
    return pl.pallas_call(
        functools.partial(
            apply_kernel, early, kinds, len(arrays) // len(kinds), quarter, len(filled), len(after)
        ),
        out_shape=[jax.ShapeDtypeStruct((count, width), BF16)] * 4
        + [jax.ShapeDtypeStruct((quarter, DH, DH), F32)] * tells,
        in_specs=[IN_SMEM]
        + [IN_VMEM] * (4 + len(partials) + len(arrays))
        + [IN_HBM] * len(filled)
        + [IN_VMEM] * len(after),
        out_specs=[IN_HBM] * 4 + [IN_VMEM] * tells,
        scratch_shapes=[
            pltpu.VMEM((count, columns), BF16),
            pltpu.VMEM((count, columns), BF16),
            pltpu.SemaphoreType.DMA((columns // (2 * DH), 2)),
        ],
        input_output_aliases={first_out + n: n for n in range(len(filled))},
        compiler_params=pltpu.CompilerParams(vmem_limit_bytes=8 * MIB),
        cost_estimate=SMALL,
        name="apply",
    )(info, *args, *partials, *arrays, *filled, *after)


def prepare_kernel(early, n_after, info, *refs):
    near, f_own, f_give, f_got, f_got_give, f_keep, f_other = refs[:7]
    s_own, s_got, s_keep, s_other = refs[7:11]
    across, mine, theirs, rest_mine, rest_theirs = refs[11 + n_after :]
    quarter = near.shape[0]
    is_kv = (info[EARLY_KV] == 1) if early else (info[EARLY_KV] != 1)
    is_first = (info[EVEN] == 1) == is_kv
    takes_near = (info[INNER] == 1) if early else (info[INNER] != 1)
    after_row = is_kv == (info[ROW] == 1)
    after_core = is_kv == (info[CORE] == 1)
    for i in range(quarter):
        val = jnp.where(takes_near, near[i], 0.0)
        keep = jnp.where(is_first, f_keep[i], s_keep[i])
        other = jnp.where(is_first, f_other[i], s_other[i])
        own = jnp.where(is_first, f_own[i], s_own[i])
        got = jnp.where(is_first, f_got[i], s_got[i])
        across[i] = val + jnp.where(after_row, 0.0, keep)
        here = val + jnp.where(after_row, other, 0.0)
        mine[i] = here + jnp.where(after_core, got, 0.0)
        theirs[i] = here + jnp.where(after_core, 0.0, own)
        own = jnp.where(is_first, f_give[i], s_own[quarter + i])
        got = jnp.where(is_first, f_got_give[i], s_got[quarter + i])
        rest_mine[i] = jnp.where(after_core, got, 0.0)
        rest_theirs[i] = jnp.where(after_core, 0.0, own)


def prepare(info, early, near, f, s, after):
    return pl.pallas_call(
        functools.partial(prepare_kernel, early, len(after)),
        out_shape=[jax.ShapeDtypeStruct(near.shape, F32)] * 5,
        in_specs=[IN_SMEM] + [IN_VMEM] * (11 + len(after)),
        out_specs=[IN_VMEM] * 5,
        compiler_params=pltpu.CompilerParams(vmem_limit_bytes=4 * MIB),
        cost_estimate=SMALL,
        name="prepare",
    )(info, near, *f, *s, *after)


def send(array, pairs):
    return lax.ppermute(array, "seq", pairs)


def plane_scan(planes, kv, qg):
    def scan(x, sign):
        def shift(x, by):
            pairs = [(a, a + sign * by) for a in range(planes) if 0 <= a + sign * by < planes]
            return send(x, spread_pairs(pairs))

        x, by = shift(x, 1), 1
        while by < planes:
            x, by = x + shift(x, by), 2 * by
        return x

    return scan(kv, 1), scan(qg, -1)


def spread_pairs(pairs):
    return [(4 * a + i, 4 * b + i) for a, b in pairs for i in range(4)]


def body(query, key_in, value, d_out):
    args = (query, key_in, value, d_out)
    count, width = query.shape
    heads = width // DH
    size, place = lax.axis_size("seq"), lax.axis_index("seq")
    planes = size // 4
    core, row, plane = place % 2, (place // 2) % 2, place // 4
    even = plane % 2 == 0
    early_kv = plane < planes // 2
    inner = (plane == 1) | (plane == 2) | (planes != 4)
    info = jnp.stack([core, row, even, early_kv, place * count, inner]).astype(jnp.int32)
    core_swap = [(i, i ^ 1) for i in range(size)]
    row_swap = [(i, i ^ 2) for i in range(size)]
    far_args = tuple(pltpu.with_memory_space_constraint(x, pltpu.HBM) for x in args)

    quarter = heads // 4
    cuts = slice(0, quarter // 2), slice(quarter // 2, quarter)

    def halves(own, got):
        return own[:quarter] + got[:quarter], own[quarter:] + got[quarter:]

    kinds = (0, 0), (0, 1), (1, 0), (1, 1)
    sib_keep, sib_give, left, right = first_state(info, far_args)
    got_give = send(sib_give, core_swap)
    got_keep = send(sib_keep, core_swap)
    own_give = own_state(info, left, right)
    f_give = own_give + got_give
    f_other = send(f_give, row_swap)
    s_sib, s_own, f_own, *args = second_states(info, far_args, (f_give,))
    f_keep = f_own + got_keep
    part_a, zero = local_part(info, args, kinds[:1], 0.0, (s_own,))
    s_got = send(s_sib, core_swap)
    s_keep, s_give = halves(s_own, s_got)
    f_total = f_keep + f_other + zero
    s_give, f_total = lax.optimization_barrier((s_give, f_total))
    s_other = send(s_give, row_swap)
    f = f_own, own_give, got_keep, got_give, f_keep, f_other
    s = s_own, s_got, s_keep, s_other
    part_b, inside = local_part(info, args, kinds[1:], 1.0, (s_give,))
    partials = part_a | part_b
    if planes == 4:
        near = send(f_total, spread_pairs([(0, 1), (1, 0), (2, 3), (3, 2)]))
        pair = jnp.where(inside > 0.0, s_keep + s_other + near, 0.0)
        middle = send(pair, spread_pairs([(1, 2), (2, 1)]) + core_swap[:4] + core_swap[-4:])
        outer = send(middle, spread_pairs([(0, 1), (1, 0), (2, 3), (3, 2)]))
        coming = middle + outer
    else:
        s_total = s_keep + s_other
        kv, qg = plane_scan(
            planes, jnp.where(even, f_total, s_total), jnp.where(even, s_total, f_total)
        )
        near = pair = jnp.where(early_kv, kv, qg)
        coming = jnp.where(early_kv, qg, kv)
    across, mine, theirs, rest_mine, rest_theirs = prepare(info, True, near, f, s, ())

    finish = functools.partial(apply_states, info, args, partials)
    kept_heads, other_heads = kinds[0::2], kinds[1::2]
    t_other = send(across, row_swap)
    t_kept = mine, send(theirs, core_swap)
    late = prepare(info, False, near, f, s, (across,))
    *outs, zero = finish(True, kept_heads, t_kept, None, (across, late[0]), True)
    t_rest = t_other + rest_mine + zero, send(t_other + rest_theirs, core_swap)

    across = coming + late[0]
    u_other = send(across, row_swap)
    u_kept = [coming[cut] + late[1][cut] for cut in cuts]
    u_kept += [send(coming[cut] + late[2][cut], core_swap) for cut in cuts]
    outs = finish(True, other_heads, t_rest, outs, (across,))
    *outs, zero = finish(False, kept_heads, u_kept, outs, (), True)
    u_rest = u_other + late[3] + zero, send(u_other + late[4], core_swap)
    outs = finish(False, other_heads, u_rest, outs)
    return tuple(outs)


def solution(mesh):
    spec = P(("group", "seq"), None)
    return jax.shard_map(
        body, mesh=mesh, in_specs=(spec,) * 4, out_specs=(spec,) * 4, check_vma=False
    )
```
